32 devices in a mesh: dp: 8 (over z, x), tensor: 4 (over y, core).
Axes of the slice: x: 2, y: 2, z: 4, core: 2. Of those that a mesh axis runs over, the one named last changes fastest.
Arguments:
- tokens: bfloat16 [8192, 2048], P('dp', 'tensor'), may hold values from -6 to 6
- cotangent: bfloat16 [8192, 2048], P('dp', 'tensor'), may hold values from -6 to 6
- lengths: int32 [8], P('dp'), may hold values from 256 to 1024, as said below
- gains: float32 [4, 2048], P(None, 'tensor')
- gain_stats: float32 [4, 2048], P(None, 'tensor'), may hold values from 2048 to 8192
- gain_roots: float32 [4, 2048], P(None, 'tensor'), may hold values from 0.0055242716 to 0.022097087
- master: float32 [4, 1024, 128, 128], P('tensor', 'dp'), may hold values from -0.125 to 0.125
- block_order: int32 [4, 1024], P('tensor'), may hold values from 0 to 1023, each once within a row
- left_stats: float32 [4, 1024, 128, 128], P('tensor', 'dp')
- right_stats: float32 [4, 1024, 128, 128], P('tensor', 'dp')
- left_roots: float32 [4, 1024, 128, 128], P('tensor', 'dp')
- right_roots: float32 [4, 1024, 128, 128], P('tensor', 'dp')
Outputs:
- block_out: bfloat16 [8192, 2048], P('dp', 'tensor')
- token_grads: bfloat16 [8192, 2048], P('dp', 'tensor')
- block_grads: float32 [4, 1024, 128, 128], P('tensor', 'dp')
- left_new: float32 [4, 1024, 128, 128], P('tensor', 'dp')
- right_new: float32 [4, 1024, 128, 128], P('tensor', 'dp')
- master_new: float32 [4, 1024, 128, 128], P('tensor', 'dp')
- gain_grads: float32 [4, 2048], P(None, 'tensor')
- gain_stats_new: float32 [4, 2048], P(None, 'tensor')
- gains_new: float32 [4, 2048], P(None, 'tensor')
The draws below stay inside these ranges and needn't reach their ends.
Inputs may be any that keep to these rules, and one draw needn't show every extreme that they name: `lengths`: one sequence of the draw has exactly 1024 tokens. `block_order`: each row names every block of its tensor shard once.
All inputs are finite; a program needn't handle non-finite values.
Results may differ from the reference program's by a relative error of at most 0.024.
The reference program's roundings to bfloat16 on the way count: a program that leaves them out, or rounds other values in their place, can miss the bound.
Values may be sent and summed in bfloat16 or wider, within the bound.
No kernel may reach another device: no remote copies, remote signals or barrier semaphores. Data moves between devices by JAX's collectives and lax.ppermute only.
A program may use at most 384 MiB of HBM per device.

```python
import math
import jax
import jax.numpy as jnp
from jax import lax

D = 2048
HEADS = 16
HD = 128
FF = 8192
BS = 128
SLOT = 1024
NSEQ = 8
TOKENS = 8192
BLOCKS = 1024
N_TENSOR = 4


def draw_lengths(key, part):
    key = jax.random.fold_in(key, 11)
    key_len, key_pick = jax.random.split(key)
    raw_draw = jax.random.randint(key_len, (NSEQ,), 0, 1024)
    squared = raw_draw * raw_draw // 1024
    lowest = SLOT // 4
    seq_lens = lowest + (SLOT - lowest) * squared // 1024
    chosen = jax.random.randint(key_pick, (), 0, NSEQ)
    return jnp.where(jnp.arange(NSEQ) == chosen, SLOT, seq_lens).astype(jnp.int32)


def draw_gains(key, part):
    key = jax.random.fold_in(key, 61)
    ratio = 3.0
    ramp = jnp.arange(D, dtype=jnp.float32) / (D - 1)
    rising = ratio ** (ramp - 0.5)
    jitter = jax.random.uniform(key, (4, D), jnp.float32, 0.85, 1.15)
    return (jitter * rising[None, :]).astype(jnp.float32)


def symmetric_blocks(key, diag_lo, diag_hi, off_size, magnitude):
    key_diag, key_off = jax.random.split(key)
    diagonal = jax.random.uniform(key_diag, (N_TENSOR, BLOCKS, BS), jnp.float32, diag_lo, diag_hi)
    offdiag = jax.random.normal(key_off, (N_TENSOR, BLOCKS, BS, BS), jnp.float32) * (off_size / BS ** 0.5)
    offdiag = 0.5 * (offdiag + jnp.swapaxes(offdiag, -1, -2))
    identity = jnp.eye(BS, dtype=jnp.float32)
    return (magnitude * (offdiag * (1.0 - identity) + diagonal[..., None] * identity)).astype(jnp.float32)


def draw_left_stats(key, part):
    key = jax.random.fold_in(key, 21)
    return symmetric_blocks(key, 1.0, 4.0, 0.3, 0.5 * BS * TOKENS)


def draw_right_stats(key, part):
    key = jax.random.fold_in(key, 31)
    return symmetric_blocks(key, 1.0, 4.0, 0.3, 0.5 * BS * TOKENS)


def draw_left_roots(key, part):
    key = jax.random.fold_in(key, 41)
    return symmetric_blocks(key, 0.5, 2.0, 0.3, (0.5 * BS * TOKENS) ** (-0.25))


def draw_right_roots(key, part):
    key = jax.random.fold_in(key, 51)
    return symmetric_blocks(key, 0.5, 2.0, 0.3, (0.5 * BS * TOKENS) ** (-0.25))


def level_of(stream_key, shape, cuts, smallest, top_value):
    def one(dim, parts):
        draws = jax.random.uniform(jax.random.fold_in(jax.random.fold_in(stream_key, 6), dim), (parts,), jnp.float32, smallest / len(cuts), top_value / len(cuts))
        return jnp.repeat(jnp.exp(draws), shape[dim] // parts).reshape((-1,) + (1,) * (len(shape) - dim - 1))

    loudness = one(*cuts[0])
    for cut in cuts[1:]:
        loudness = loudness * one(*cut)
    return loudness


def scatter_about(key, shape, width, limit, cuts=(), kind=jnp.bfloat16):
    drawn = width * jax.random.normal(key, shape, jnp.float32)
    if cuts:
        drawn = drawn * level_of(key, shape, cuts, -0.22, 0.18)
    return jnp.clip(drawn, -limit, limit).astype(kind)


def setup_inputs(seed: int = 0) -> dict:
    splits = jax.random.split(jax.random.key(seed), 13)
    return {
        "tokens": scatter_about(splits[0], (TOKENS, D), 1.0, 6.0, ((0, 8), (1, 4))),
        "cotangent": scatter_about(splits[1], (TOKENS, D), 1.0, 6.0, ((0, 8), (1, 4))),
        "lengths": draw_lengths(jax.random.fold_in(splits[12], 71), 0),
        "gains": draw_gains(jax.random.fold_in(splits[12], 71), 0),
        "gain_stats": jnp.clip(jnp.exp(math.log(8192.0) - 1.3862944 * jax.random.uniform(splits[4], (4, D), jnp.float32) ** level_of(splits[4], (4, D), ((1, 4),), -0.2, 0.2)), 2048.0, 8192.0),
        "gain_roots": jnp.clip(jnp.exp(math.log(0.022097087) - 1.3862944 * jax.random.uniform(splits[5], (4, D), jnp.float32) ** level_of(splits[5], (4, D), ((1, 4),), -0.2, 0.2)), 0.0055242716, 0.022097087),
        "master": scatter_about(splits[6], (N_TENSOR, BLOCKS, BS, BS), D ** -0.5, 0.125, ((0, 4), (1, 8)), jnp.float32),
        "block_order": jax.vmap(lambda own: jax.random.permutation(own, BLOCKS))(jax.random.split(splits[7], N_TENSOR)).reshape((N_TENSOR, BLOCKS)).astype(jnp.int32),
        "left_stats": draw_left_stats(jax.random.fold_in(splits[12], 71), 0),
        "right_stats": draw_right_stats(jax.random.fold_in(splits[12], 71), 0),
        "left_roots": draw_left_roots(jax.random.fold_in(splits[12], 71), 0),
        "right_roots": draw_right_roots(jax.random.fold_in(splits[12], 71), 0),
    }


@jax.custom_vjp
def low(v):
    return lax.optimization_barrier(v.astype(jnp.bfloat16)).astype(jnp.float32)

@jax.custom_vjp
def low_back(v):
    return v

def low_keep(v):
    return (low(v), None)

def low_pass(kept, grad):
    return (grad,)

def back_keep(v):
    return (v, None)

def back_low(kept, grad):
    return (low(grad),)
low.defvjp(low_keep, low_pass)
low_back.defvjp(back_keep, back_low)
EPSILON = 1e-06
THETA = 500000.0
DECAY = 0.5
LEARN_RATE = 0.25
GAIN_RATE = 0.2
HIGHEST_PREC = lax.Precision.HIGHEST

def to_blocks(matrix, size_b):
    row_count, col_count = matrix.shape
    return matrix.reshape(row_count // size_b, size_b, col_count // size_b, size_b).transpose(0, 2, 1, 3).reshape(-1, size_b, size_b)

def from_blocks(blocks, row_count, col_count, size_b):
    return blocks.reshape(row_count // size_b, col_count // size_b, size_b, size_b).transpose(0, 2, 1, 3).reshape(row_count, col_count)

def stack_shapes(width_d, hidden_local, width_local):
    return [(width_d, width_local)] * 3 + [(width_local, width_d)] + [(width_d, hidden_local)] * 2 + [(hidden_local, width_d)]

def split_stack(stack, width_d, hidden_local, width_local, size_b):
    matrices = []
    offset = 0
    for row_count, col_count in stack_shapes(width_d, hidden_local, width_local):
        count_b = row_count // size_b * (col_count // size_b)
        matrices.append(from_blocks(stack[offset:offset + count_b], row_count, col_count, size_b))
        offset = offset + count_b
    return matrices

def join_stack(matrices, size_b):
    return jnp.concatenate([to_blocks(matrix, size_b) for matrix in matrices], axis=0)

def rope_tables(seq_len, head_dim):
    half_dim = head_dim // 2
    freqs = THETA ** (-(2.0 * jnp.arange(half_dim, dtype=jnp.float32)) / head_dim)
    angles = jnp.arange(seq_len, dtype=jnp.float32)[:, None] * freqs[None, :]
    return (jnp.cos(angles)[:, None, :], jnp.sin(angles)[:, None, :])

def rotary(values, cos_t, sin_t):
    half_dim = values.shape[-1] // 2
    first_half = values[..., :half_dim]
    second_half = values[..., half_dim:]
    return jnp.concatenate([first_half * cos_t - second_half * sin_t, second_half * cos_t + first_half * sin_t], axis=-1)

def norm_rows(matrix, gain_row):
    return matrix * lax.rsqrt(lax.optimization_barrier(jnp.mean(matrix * matrix, axis=-1, keepdims=True)) + EPSILON) * gain_row

def matmul_hi(left, right):
    return jnp.dot(left, right, precision=HIGHEST_PREC, preferred_element_type=jnp.float32)

def layer_seq(seq_rows, length, weights_low, gain_low):
    proj_q, proj_k, proj_v, proj_o, proj_gate, proj_up, proj_down = weights_low
    cos_t, sin_t = rope_tables(SLOT, HD)
    queries = low_back(matmul_hi(seq_rows, proj_q))
    keys_raw = low_back(matmul_hi(seq_rows, proj_k))
    values_raw = low_back(matmul_hi(seq_rows, proj_v))
    queries = norm_rows(queries, gain_low[0])
    keys_raw = norm_rows(keys_raw, gain_low[1])
    q_low = low(rotary(queries.reshape(SLOT, HEADS, HD), cos_t, sin_t))
    k_low = low(rotary(keys_raw.reshape(SLOT, HEADS, HD), cos_t, sin_t))
    v_low = low(values_raw).reshape(SLOT, HEADS, HD)
    scores = low_back(jnp.einsum('qhd,khd->hqk', q_low, k_low, precision=HIGHEST_PREC) * HD ** (-0.5))
    positions = jnp.arange(SLOT)
    allowed = (positions[None, :] <= positions[:, None]) & (positions[None, :] < length)
    scores = jnp.where(allowed[None], scores, -1e+30)
    attn_probs = jax.nn.softmax(scores, axis=-1)
    attn_vals = jnp.einsum('hqk,khd->qhd', low(attn_probs), v_low, precision=HIGHEST_PREC).reshape(SLOT, D)
    attn_low = low(low_back(attn_vals))
    branch = low_back(matmul_hi(attn_low, proj_o))
    hidden_state = seq_rows + norm_rows(branch, gain_low[2])
    hidden_low = low(hidden_state)
    gate_act = low_back(matmul_hi(hidden_low, proj_gate))
    up_act = low_back(matmul_hi(hidden_low, proj_up))
    inner_act = low(jax.nn.silu(gate_act) * up_act)
    mlp_out = low_back(matmul_hi(inner_act, proj_down))
    return hidden_state + norm_rows(mlp_out, gain_low[3])

def reference(tokens, cotangent, lengths, gains, gain_stats, gain_roots, master, block_order, left_stats, right_stats, left_roots, right_roots):
    width_local = D // N_TENSOR
    hidden_local = FF // N_TENSOR

    def unpermute(slots_w, order_row):
        return jnp.zeros_like(slots_w).at[order_row].set(slots_w)

    def permute(stack, order_row):
        return stack[order_row]

    def split_one(stack):
        return split_stack(stack, D, hidden_local, width_local, BS)

    def join_one(q_part, k_part, v_part, o_part, gate_part, up_part, down_part):
        return join_stack([q_part, k_part, v_part, o_part, gate_part, up_part, down_part], BS)
    local_stacks = jax.vmap(unpermute)(master, block_order)
    pieces = jax.vmap(split_one)(local_stacks)
    proj_q = jnp.transpose(pieces[0], (1, 0, 2)).reshape(D, D)
    proj_k = jnp.transpose(pieces[1], (1, 0, 2)).reshape(D, D)
    proj_v = jnp.transpose(pieces[2], (1, 0, 2)).reshape(D, D)
    proj_o = pieces[3].reshape(D, D)
    proj_gate = jnp.transpose(pieces[4], (1, 0, 2)).reshape(D, FF)
    proj_up = jnp.transpose(pieces[5], (1, 0, 2)).reshape(D, FF)
    proj_down = pieces[6].reshape(FF, D)
    weights_f = (proj_q, proj_k, proj_v, proj_o, proj_gate, proj_up, proj_down)
    x_all = tokens.astype(jnp.float32).reshape(NSEQ, SLOT, D)
    positions = jnp.arange(SLOT)
    live_rows = (positions[None, :] < lengths[:, None]).astype(jnp.float32)
    cot_all = cotangent.astype(jnp.float32).reshape(NSEQ, SLOT, D) * live_rows[:, :, None]

    def forward(x_in, weights_in, gains_in):
        weights_low = tuple((low(weight) for weight in weights_in))
        gain_low = low(gains_in)
        checked = jax.checkpoint(layer_seq)

        def one_seq(item):
            return checked(item[0], item[1], weights_low, gain_low)
        return lax.map(one_seq, (x_in, lengths))
    outputs, pull_back = jax.vjp(forward, x_all, weights_f, gains)
    d_x, d_weights, d_gains = pull_back(cot_all)
    block_out = outputs.reshape(TOKENS, D).astype(jnp.bfloat16)
    token_grads = d_x.reshape(TOKENS, D).astype(jnp.bfloat16)
    g_q = jnp.transpose(d_weights[0].reshape(D, N_TENSOR, width_local), (1, 0, 2))
    g_k = jnp.transpose(d_weights[1].reshape(D, N_TENSOR, width_local), (1, 0, 2))
    g_v = jnp.transpose(d_weights[2].reshape(D, N_TENSOR, width_local), (1, 0, 2))
    g_o = d_weights[3].reshape(N_TENSOR, width_local, D)
    g_gate = jnp.transpose(d_weights[4].reshape(D, N_TENSOR, hidden_local), (1, 0, 2))
    g_up = jnp.transpose(d_weights[5].reshape(D, N_TENSOR, hidden_local), (1, 0, 2))
    g_down = d_weights[6].reshape(N_TENSOR, hidden_local, D)
    grad_stacks = jax.vmap(join_one)(g_q, g_k, g_v, g_o, g_gate, g_up, g_down)
    block_grads = jax.vmap(permute)(grad_stacks, block_order)
    left_new = DECAY * left_stats + (1.0 - DECAY) * jnp.einsum('tbij,tbkj->tbik', block_grads, block_grads, precision=HIGHEST_PREC)
    right_new = DECAY * right_stats + (1.0 - DECAY) * jnp.einsum('tbji,tbjk->tbik', block_grads, block_grads, precision=HIGHEST_PREC)
    left_part = jnp.einsum('tbij,tbjk->tbik', left_roots, block_grads, precision=HIGHEST_PREC)
    precond = jnp.einsum('tbij,tbjk->tbik', left_part, right_roots, precision=HIGHEST_PREC)
    master_new = master - LEARN_RATE * precond
    gain_stats_new = DECAY * gain_stats + (1.0 - DECAY) * d_gains * d_gains
    gains_new = gains - GAIN_RATE * d_gains * gain_roots
    return (block_out, token_grads, block_grads, left_new, right_new, master_new, d_gains, gain_stats_new, gains_new)
```

```python
import jax
import jax.numpy as jnp
import numpy as np
from jax import lax
from jax.experimental import pallas as pl
from jax.experimental.pallas import tpu as pltpu
from jax.sharding import PartitionSpec as P

HEADS = 16
HD = 128
FF = 8192
EPSILON = 1e-06
THETA = 500000.0
DECAY = 0.5
LEARN_RATE = 0.25
GAIN_RATE = 0.2
NEG = -1e30
MIB = 1024 * 1024
f32 = jnp.float32
bf16 = jnp.bfloat16


def after(value, *others):
    return lax.optimization_barrier((value,) + others)[0]


class Links:
    def __init__(self):
        self.n_dp = lax.axis_size("dp")
        self.n_t = lax.axis_size("tensor")
        self.nz = self.n_dp // 2
        self.ny = self.n_t // 2
        self.d = lax.axis_index("dp")
        self.z, self.x = self.d // 2, self.d % 2
        self.t = lax.axis_index("tensor")
        self.y, self.c = self.t // 2, self.t % 2
        self.z_groups = [[2 * z + x for z in range(self.nz)] for x in range(2)]

    def ring(self, value):
        pairs = [(2 * z + x, 2 * ((z - 1) % self.nz) + x) for z in range(self.nz) for x in range(2)]
        return lax.ppermute(value, "dp", pairs)

    def gather_z(self, value):
        return lax.all_gather(value, "dp", axis=0, tiled=True, axis_index_groups=self.z_groups)

    def reduce_z(self, value):
        return lax.psum_scatter(
            value, "dp", scatter_dimension=0, tiled=True, axis_index_groups=self.z_groups
        )

    def swap_x(self, value):
        return lax.ppermute(value, "dp", [(i, i ^ 1) for i in range(self.n_dp)])

    def swap_core(self, value):
        return lax.ppermute(value, "tensor", [(i, i ^ 1) for i in range(self.n_t)])

    def shift_y(self, value, step):
        pairs = [(i, 2 * ((i // 2 + step) % self.ny) + i % 2) for i in range(self.n_t)]
        return lax.ppermute(value, "tensor", pairs)

    def shift_t(self, value, step):
        return lax.ppermute(value, "tensor", [(i, (i + step) % self.n_t) for i in range(self.n_t)])

    def gather_rows(self, own, meanwhile=None):
        rows = own.shape[0]
        pieces = [(self.y, own)]
        for step in range(1, self.ny):
            pieces.append(((self.y + self.ny - step) % self.ny, self.shift_y(own, step)))
        parts, places = [], []
        for row_y, piece in pieces:
            parts += [piece, self.swap_core(piece)]
            places += [2 * row_y + self.c, 2 * row_y + 1 - self.c]
        if meanwhile is not None:
            parts[-1] = after(parts[-1], *meanwhile(own))
        return stack_rows(parts, jnp.stack(places))

    def reduce_rows(self, part, meanwhile=None):
        rows = part.shape[0] // self.n_t
        cut = part.reshape((self.ny, 2, rows, part.shape[1]))
        got = self.swap_core(lax.dynamic_index_in_dim(cut, 1 - self.c, 1, False))
        kept = lax.dynamic_index_in_dim(cut, self.c, 1, False)
        both = (kept.astype(f32) + got.astype(f32)).astype(bf16)
        total = lax.dynamic_index_in_dim(both, self.y, 0, False).astype(f32)
        for step in range(1, self.ny):
            piece = lax.dynamic_index_in_dim(both, (self.y + step) % self.ny, 0, False)
            got = self.shift_y(piece, step)
            if meanwhile is not None and step == 1:
                got = after(got, *meanwhile(both))
            total = total + got.astype(f32)
        return total

    def rows_to_cols(self, own):
        rows, width = own.shape[0], own.shape[1] // self.n_t
        full = jnp.zeros((rows * self.n_t, width), own.dtype)
        for step in range(self.n_t):
            piece = lax.dynamic_slice_in_dim(own, ((self.t + step) % self.n_t) * width, width, 1)
            if step:
                piece = self.shift_t(piece, step)
            row0 = ((self.t + self.n_t - step) % self.n_t) * rows
            full = lax.dynamic_update_slice_in_dim(full, piece, row0, 0)
        return full


def fit(count, most=8):
    return next(step for step in (8, 4, 2, 1) if step <= most and count % step == 0)


def stack_rows(parts, places):
    rows, cols = parts[0].shape
    n = len(parts)

    def kernel(places_ref, *refs):
        out, sem = refs[n], refs[n + 1]
        copies = []
        for i in range(n):
            start = pl.multiple_of(places_ref[i] * rows, rows)
            copies.append(pltpu.make_async_copy(refs[i], out.at[pl.ds(start, rows), :], sem.at[i]))
            copies[-1].start()
        for copy in copies:
            copy.wait()

    return pl.pallas_call(
        kernel,
        grid_spec=pltpu.PrefetchScalarGridSpec(
            num_scalar_prefetch=1,
            grid=(1,),
            in_specs=[pl.BlockSpec(memory_space=pl.ANY)] * n,
            out_specs=pl.BlockSpec(memory_space=pltpu.VMEM),
            scratch_shapes=[pltpu.SemaphoreType.DMA((n,))],
        ),
        out_shape=jax.ShapeDtypeStruct((n * rows, cols), parts[0].dtype),
        compiler_params=pltpu.CompilerParams(vmem_limit_bytes=32 * MIB),
        name="stack_rows",
    )(places, *parts)


def sorted_tiles(master, perm, lo, hi):
    size_b = master.shape[-1]
    step = fit(hi - lo)

    def kernel(perm_ref, *refs):
        for j in range(step):
            refs[step][j] = refs[j][0].astype(bf16)

    def spec(j):
        return pl.BlockSpec((1, size_b, size_b), lambda i, p: (p[lo + step * i + j], 0, 0))

    return pl.pallas_call(
        kernel,
        grid_spec=pltpu.PrefetchScalarGridSpec(
            num_scalar_prefetch=1,
            grid=((hi - lo) // step,),
            in_specs=[spec(j) for j in range(step)],
            out_specs=pl.BlockSpec((step, size_b, size_b), lambda i, p: (i, 0, 0)),
        ),
        out_shape=jax.ShapeDtypeStruct((hi - lo, size_b, size_b), bf16),
        name="sorted_tiles",
    )(perm, *([master] * step))


def place_tiles(sources, parts, shapes, ids, counts, size_b):
    arrays = []
    for source in sources:
        if not any(source[0] is array for array in arrays):
            arrays.append(source[0])
    places = [next(i for i, array in enumerate(arrays) if array is source[0]) for source in sources]
    n_src, n_out = len(arrays), len(shapes)

    def kernel(ids_ref, counts_ref, *refs):
        outs, sem = refs[n_src : n_src + n_out], refs[-1]
        for m, edge, base, cols, off in parts:
            for s, (_, at, row, lo, hi) in zip(places, sources):

                def step(k, carry, s=s, m=m, base=base, cols=cols, off=off, row=row, skip=lo - at):
                    tile = ids_ref[row, k] - base
                    r = tile // cols
                    c = tile - r * cols + off
                    pltpu.make_async_copy(
                        refs[s].at[k - skip],
                        outs[m].at[
                            pl.ds(pl.multiple_of(r * size_b, size_b), size_b),
                            pl.ds(pl.multiple_of(c * size_b, size_b), size_b),
                        ],
                        sem,
                    ).start()
                    return carry

                first = jnp.maximum(counts_ref[row, edge], lo)
                last = jnp.minimum(counts_ref[row, edge + 1], hi)
                lax.fori_loop(first, last, step, 0)
        for out in outs:
            pltpu.make_async_copy(out, out, sem).wait()

    return pl.pallas_call(
        kernel,
        grid_spec=pltpu.PrefetchScalarGridSpec(
            num_scalar_prefetch=2,
            grid=(1,),
            in_specs=[pl.BlockSpec(memory_space=pl.ANY)] * n_src,
            out_specs=[pl.BlockSpec(memory_space=pltpu.VMEM)] * n_out,
            scratch_shapes=[pltpu.SemaphoreType.DMA],
        ),
        out_shape=[jax.ShapeDtypeStruct(shape, bf16) for shape in shapes],
        compiler_params=pltpu.CompilerParams(vmem_limit_bytes=60 * MIB),
        name="place_tiles",
    )(ids, counts, *arrays)


def pick_tiles(matrices, parts, ids, counts, rows, lo, hi, size_b):
    n_src, n_out = len(matrices), len(rows)

    def kernel(ids_ref, counts_ref, *refs):
        outs, sem = refs[n_src : n_src + n_out], refs[-1]
        for m, edge, base, cols, off in parts:
            for i, group in enumerate(rows):
                for j, row in enumerate(group):

                    def step(k, carry, i=i, j=j, row=row, m=m, base=base, cols=cols, off=off):
                        tile = ids_ref[row, k] - base
                        r = tile // cols
                        c = tile - r * cols + off
                        pltpu.make_async_copy(
                            refs[m].at[
                                pl.ds(pl.multiple_of(r * size_b, size_b), size_b),
                                pl.ds(pl.multiple_of(c * size_b, size_b), size_b),
                            ],
                            outs[i].at[j, k - lo],
                            sem,
                        ).start()
                        return carry

                    first = jnp.maximum(counts_ref[row, edge], lo)
                    last = jnp.minimum(counts_ref[row, edge + 1], hi)
                    lax.fori_loop(first, last, step, 0)
        for out in outs:
            pltpu.make_async_copy(out, out, sem).wait()

    return pl.pallas_call(
        kernel,
        grid_spec=pltpu.PrefetchScalarGridSpec(
            num_scalar_prefetch=2,
            grid=(1,),
            in_specs=[pl.BlockSpec(memory_space=pl.ANY)] * n_src,
            out_specs=[pl.BlockSpec(memory_space=pltpu.VMEM)] * n_out,
            scratch_shapes=[pltpu.SemaphoreType.DMA],
        ),
        out_shape=[jax.ShapeDtypeStruct((len(group), hi - lo, size_b, size_b), bf16) for group in rows],
        compiler_params=pltpu.CompilerParams(vmem_limit_bytes=60 * MIB),
        name="pick_tiles",
    )(ids, counts, *matrices)


def dot_nt(a, b):
    return lax.dot_general(a, b, (((1,), (1,)), ((), ())), preferred_element_type=f32)


def dot_tn(a, b):
    return lax.dot_general(a, b, (((0,), (0,)), ((), ())), preferred_element_type=f32)


def dot_nn(a, b):
    return lax.dot_general(a, b, (((1,), (0,)), ((), ())), preferred_element_type=f32)


def softmax_block(q_block, k_head, first, length):
    keys = k_head.shape[0]
    scores = dot_nt(q_block, k_head) * (HD**-0.5)
    rows = first + lax.broadcasted_iota(jnp.int32, scores.shape, 0)
    cols = lax.broadcasted_iota(jnp.int32, scores.shape, 1)
    scores = jnp.where((cols <= rows) & (cols < length), scores, NEG)
    probs = jnp.exp(scores - jnp.max(scores, axis=-1, keepdims=True))
    return probs / jnp.sum(probs, axis=-1, keepdims=True)


def attention(raw, scale_q, scale_k, gains, cos_t, sin_t, lengths):
    slots, width = raw.shape[0], raw.shape[1] // 3
    heads = width // HD
    block = min(256, slots)

    def kernel(len_ref, q_ref, k_ref, v_ref, sq_ref, sk_ref, gain_ref, cos_ref, sin_ref, out_ref, ql_ref, kl_ref, vl_ref):
        def turned(ref, scale, row):
            val = ref[...] * scale[...] * gain_ref[row : row + 1, :]
            return (val * cos_ref[...] + pltpu.roll(val, HD // 2, 1) * sin_ref[...]).astype(bf16)

        ql_ref[...] = turned(q_ref, sq_ref, 0)
        kl_ref[...] = turned(k_ref, sk_ref, 1)
        vl_ref[...] = v_ref[...].astype(bf16)
        for first in range(0, slots, block):
            last = first + block
            probs = softmax_block(ql_ref[first:last, :], kl_ref[:last, :], first, len_ref[0])
            out_ref[first:last, :] = dot_nn(probs.astype(bf16), vl_ref[:last, :]).astype(bf16)

    def head_spec(part):
        return pl.BlockSpec((slots, HD), lambda h, n: (0, part * heads + h))

    whole = lambda shape: pl.BlockSpec(shape, lambda h, n: (0, 0))
    out_spec = pl.BlockSpec((slots, HD), lambda h, n: (0, h))
    return pl.pallas_call(
        kernel,
        grid_spec=pltpu.PrefetchScalarGridSpec(
            num_scalar_prefetch=1,
            grid=(heads,),
            in_specs=[head_spec(0), head_spec(1), head_spec(2), whole((slots, 1)), whole((slots, 1))]
            + [pl.BlockSpec((4, HD), lambda h, n: (0, h)), whole((slots, HD)), whole((slots, HD))],
            out_specs=[out_spec] * 4,
        ),
        out_shape=[jax.ShapeDtypeStruct((slots, width), bf16)] * 4,
        compiler_params=pltpu.CompilerParams(vmem_limit_bytes=48 * MIB),
        name="attention",
    )(lengths, raw, raw, raw, scale_q, scale_k, gains, cos_t, sin_t)


def attention_back(q_low, k_low, v_low, d_attn, cos_t, sin_t, lengths):
    slots, width = q_low.shape
    heads = width // HD
    block = min(256, slots)

    def kernel(len_ref, q_ref, k_ref, v_ref, do_ref, cos_ref, sin_ref, dq_ref, dk_ref, dv_ref, dk_acc, dv_acc):
        def turned_back(val, rows):
            return val * cos_ref[rows, :] - pltpu.roll(val, HD // 2, 1) * sin_ref[rows, :]

        dk_acc[...] = jnp.zeros_like(dk_acc)
        dv_acc[...] = jnp.zeros_like(dv_acc)
        for first in range(0, slots, block):
            last = first + block
            rows, keys = slice(first, last), slice(0, last)
            probs = softmax_block(q_ref[rows, :], k_ref[keys, :], first, len_ref[0])
            d_out = do_ref[rows, :]
            d_probs = dot_nt(d_out, v_ref[keys, :])
            delta = jnp.sum(probs * d_probs, axis=-1, keepdims=True)
            d_scores = (probs * (d_probs - delta)).astype(bf16)
            dq_ref[rows, :] = turned_back(dot_nn(d_scores, k_ref[keys, :]) * (HD**-0.5), rows)
            dk_acc[keys, :] += dot_tn(d_scores, q_ref[rows, :])
            dv_acc[keys, :] += dot_tn(probs.astype(bf16), d_out)
        dk_ref[...] = turned_back(dk_acc[...] * (HD**-0.5), slice(0, slots))
        dv_ref[...] = dv_acc[...].astype(bf16)

    spec = pl.BlockSpec((slots, HD), lambda h, n: (0, h))
    whole = pl.BlockSpec((slots, HD), lambda h, n: (0, 0))
    return pl.pallas_call(
        kernel,
        grid_spec=pltpu.PrefetchScalarGridSpec(
            num_scalar_prefetch=1,
            grid=(heads,),
            in_specs=[spec] * 4 + [whole] * 2,
            out_specs=[spec] * 3,
            scratch_shapes=[pltpu.VMEM((slots, HD), f32)] * 2,
        ),
        out_shape=[
            jax.ShapeDtypeStruct((slots, width), f32),
            jax.ShapeDtypeStruct((slots, width), f32),
            jax.ShapeDtypeStruct((slots, width), bf16),
        ],
        compiler_params=pltpu.CompilerParams(vmem_limit_bytes=48 * MIB),
        name="attention_back",
    )(lengths, q_low, k_low, v_low, d_attn, cos_t, sin_t)


def renew(grads, perm, lo, held, outs):
    count, size_b = grads.shape[0], grads.shape[-1]
    n_old = 0 if outs is None else len(outs)
    batch = fit(count)
    steps = count // batch

    def kernel(perm_ref, g_ref, *refs):
        ins = [refs[a * batch : (a + 1) * batch] for a in range(5)]
        outs_ref = refs[5 * batch + n_old : 5 * batch + n_old + 4]
        held_ref, sems = refs[-2:]
        i = pl.program_id(0)
        side = i % 2

        def drain(which):
            pltpu.make_async_copy(held_ref.at[which], held_ref.at[which], sems.at[which]).wait()

        @pl.when(i >= 2)
        def _():
            drain(side)

        for j in range(batch):
            master, left_s, right_s, left_r, right_r = (ins[a][j][0] for a in range(5))
            g = g_ref[j]
            held_ref[side, 0, j] = g.astype(f32)
            held_ref[side, 1, j] = DECAY * left_s + (1.0 - DECAY) * dot_nt(g, g)
            held_ref[side, 2, j] = DECAY * right_s + (1.0 - DECAY) * dot_tn(g, g)
            left = dot_nn(left_r.astype(bf16), g).astype(bf16)
            held_ref[side, 3, j] = master - LEARN_RATE * dot_nn(left, right_r.astype(bf16))
        for j in range(batch):
            slot = perm_ref[lo + batch * i + j]
            for a in range(4):
                pltpu.make_async_copy(held_ref.at[side, a, j], outs_ref[a].at[slot], sems.at[side]).start()

        @pl.when(i == steps - 1)
        def _():
            drain(side)
            if steps > 1:
                drain(1 - side)

    def spec(j):
        return pl.BlockSpec((1, size_b, size_b), lambda i, p: (p[lo + batch * i + j], 0, 0))

    return pl.pallas_call(
        kernel,
        grid_spec=pltpu.PrefetchScalarGridSpec(
            num_scalar_prefetch=1,
            grid=(steps,),
            in_specs=[pl.BlockSpec((batch, size_b, size_b), lambda i, p: (i, 0, 0))]
            + [spec(j) for _ in range(5) for j in range(batch)]
            + [pl.BlockSpec(memory_space=pl.ANY)] * n_old,
            out_specs=[pl.BlockSpec(memory_space=pl.ANY)] * 4,
            scratch_shapes=[
                pltpu.VMEM((2, 4, batch, size_b, size_b), f32),
                pltpu.SemaphoreType.DMA((2,)),
            ],
        ),
        out_shape=[jax.ShapeDtypeStruct(held[0].shape, f32)] * 4,
        input_output_aliases={2 + 5 * batch + i: i for i in range(n_old)},
        name="renew",
    )(perm, grads, *[array for array in held for _ in range(batch)], *(outs or ()))


def rope_tables(seq_len):
    half = HD // 2
    freqs = THETA ** (-(2.0 * jnp.arange(half, dtype=f32)) / HD)
    angles = jnp.arange(seq_len, dtype=f32)[:, None] * freqs[None, :]
    cos_t, sin_t = jnp.cos(angles), jnp.sin(angles)
    return jnp.concatenate([cos_t, cos_t], 1), jnp.concatenate([-sin_t, sin_t], 1)


def core(fast, cuts, links, tables, perm, gain_full, args):
    tokens, cotangent, lengths, gains, gain_stats, gain_roots = args[:6]
    master, left_stats, right_stats, left_roots, right_roots = args[6:]
    ids, counts = tables
    size_b = master.shape[-1]
    slots, width_local = tokens.shape
    n_t = links.n_t
    width_d = width_local * n_t
    hidden_local = FF // n_t
    count = master.shape[0]

    edges, cols_w, cols_h, cols_d = tile_edges(width_local, width_d, hidden_local, size_b)
    qkv_parts = [(i, edges[i], cols_w, i * cols_w) for i in range(3)]
    o_part, gate_part, up_part, down_part = (
        (3 + i, edges[3 + i], cols, 0) for i, cols in enumerate((cols_d, cols_h, cols_h, cols_d))
    )

    edge_a, edge_b1, edge_b, count = cuts["a"], cuts["b1"], cuts["b"], cuts["end"]
    own_a = sorted_tiles(master, perm, 0, edge_a)
    later = after(perm, own_a)
    owns = [sorted_tiles(master, later, lo, hi) for lo, hi in ((edge_a, edge_b1), (edge_b1, edge_b), (edge_b, count))]
    tok_full = lax.all_gather(tokens, "tensor", axis=1, tiled=True)
    cot_full = lax.all_gather(cotangent, "tensor", axis=1, tiled=True)

    mine, theirs = [own_a], [links.swap_x(own_a)]
    for r in range(1, links.nz):
        if r == 1:
            mine.append(links.ring(own_a))
        else:
            mine.append(links.ring(after(mine[-1], theirs[r - 2], *(owns if r == 2 else ()))))
        if r > 1:
            theirs.append(links.swap_x(after(mine[r - 1], theirs[-1])))
    theirs.append(links.swap_x(after(mine[-1], theirs[-1])))
    own_b1 = links.swap_x(after(owns[0], theirs[-1]))
    own_c = links.swap_x(after(owns[2], own_b1))
    own_b2 = links.swap_x(after(owns[1], own_b1))
    sources_a = []
    for r in range(links.nz):
        sources_a.append((mine[r], 0, 2 * r, 0, edge_a))
        sources_a.append((theirs[r], 0, 2 * r + 1, 0, edge_a))

    def matrices(sources, groups, shapes):
        return place_tiles(sources, [(m,) + part for m, part in groups], shapes, ids, counts, size_b)

    def send_others(gathered, n, last):
        sent = []
        for r in range(1, links.nz):
            piece = lax.dynamic_slice_in_dim(gathered, ((links.z + r) % links.nz) * n, n, 0)
            last = links.swap_x(after(piece, last))
            sent.append(last)
        return sent

    def all_sources(lo, hi, gathered, own_x, rest_x):
        n = hi - lo
        found = [(gathered, z * n, links.n_dp + 2 * z, lo, hi) for z in range(links.nz)]
        found.append((own_x, 0, 1, lo, hi))
        return found + [(rest_x[r - 1], 0, 2 * r + 1, lo, hi) for r in range(1, links.nz)]

    n_b1, n_b2, n_c = edge_b1 - edge_a, edge_b - edge_b1, count - edge_b
    z_b1, z_b2, z_c = (
        links.gather_z(after(own, mine[-1], theirs[-2])) for own in (owns[0], owns[1], jnp.concatenate([owns[2], own_c], axis=0))
    )
    rest_b1 = send_others(z_b1, n_b1, own_b2)
    rest_b2 = send_others(z_b2, n_b2, rest_b1[-1])
    sources_b1 = sources_a + all_sources(edge_a, edge_b1, z_b1, own_b1, rest_b1)
    sources_b2 = sources_b1 + all_sources(edge_b1, edge_b, z_b2, own_b2, rest_b2)
    sources_c = sources_b2 + [
        (z_c, (2 * z + xr) * n_c, links.n_dp + 2 * z + xr, edge_b, count) for z in range(links.nz) for xr in range(2)
    ]
    if not fast:
        sources_a = sources_b1 = sources_b2 = sources_c

    gain_local = gains.astype(bf16).astype(f32)
    length = lengths[0]
    cos_t, sin_t = rope_tables(slots)
    own_rows = slots // n_t
    row0 = links.t * own_rows
    tok_rows = lax.dynamic_slice_in_dim(tok_full, row0, own_rows, 0).astype(f32)
    live = (row0 + jnp.arange(own_rows) < length).astype(f32)[:, None]
    grad_rows = lax.dynamic_slice_in_dim(cot_full, row0, own_rows, 0).astype(f32) * live

    w_qkv, w_o = matrices(
        sources_a,
        [(0, part) for part in qkv_parts] + [(1, o_part)],
        [(width_d, 3 * width_local), (width_local, width_d)],
    )
    raw = after(dot_nn(tok_full, w_qkv), own_b1)
    queries, keys_raw = raw[:, :width_local], raw[:, width_local : 2 * width_local]
    squares = lax.psum(
        jnp.stack([jnp.sum(queries * queries, axis=-1), jnp.sum(keys_raw * keys_raw, axis=-1)]), "tensor"
    )
    scale_q = lax.rsqrt(squares[0] / width_d + EPSILON)[:, None]
    scale_k = lax.rsqrt(squares[1] / width_d + EPSILON)[:, None]
    attn_low, q_low, k_low, v_low = attention(raw, scale_q, scale_k, gain_local, cos_t, sin_t, lengths)
    branch = links.reduce_rows(dot_nn(after(attn_low, own_c, own_b2), w_o).astype(bf16))
    branch = after(branch, z_b1)
    rms_a = lax.rsqrt(jnp.mean(branch * branch, axis=-1, keepdims=True) + EPSILON)
    hidden_rows = tok_rows + branch * rms_a * gain_full[2]
    hidden_low = links.gather_rows(hidden_rows.astype(bf16))
    hidden_low = after(hidden_low, rest_b1[0])

    (w_gate,) = matrices(sources_b1, [(0, gate_part)], [(width_d, hidden_local)])
    gate_act = dot_nn(hidden_low, w_gate)
    sig_gate = jax.nn.sigmoid(gate_act)
    silu_act = gate_act * sig_gate
    (w_down,) = matrices(sources_c, [(0, down_part)], [(hidden_local, width_d)])
    sources_b2 = [(after(sources_b2[0][0], w_down),) + sources_b2[0][1:]] + sources_b2[1:]
    (w_up,) = matrices(sources_b2, [(0, up_part)], [(width_d, hidden_local)])
    up_act = dot_nn(hidden_low, w_up)
    inner_low = (silu_act * up_act).astype(bf16)
    mlp_rows = links.reduce_rows(dot_nn(inner_low, w_down).astype(bf16))
    rms_m = lax.rsqrt(jnp.mean(mlp_rows * mlp_rows, axis=-1, keepdims=True) + EPSILON)
    result = hidden_rows + mlp_rows * rms_m * gain_full[3]
    scaled_m = gain_full[3] * grad_rows
    d_mlp = rms_m * scaled_m - mlp_rows * rms_m**3 * jnp.mean(scaled_m * mlp_rows, axis=-1, keepdims=True)
    d_mlp_low = links.gather_rows(d_mlp.astype(bf16))

    grads = {}
    grad_parts = [(0, down_part), (1, up_part), (2, gate_part), (3, o_part)] + [(4, p) for p in qkv_parts]
    held = (master, left_stats, right_stats, left_roots, right_roots)
    half_z = links.nz // 2
    edge_m = (edge_a + edge_b1) // 4 * 2
    abs_row = lambda z, xr: links.n_dp + 2 * z + xr
    theirs_rows = [[abs_row(z, 1) for z in range(half_z)], [abs_row(z, 1) for z in range(half_z, links.nz)]]
    mine_rows = [abs_row(z, 0) for z in range(links.nz)]

    def cut_out(lo, hi, n_mats, rows):
        parts = [(m,) + part for m, part in grad_parts if m < n_mats]
        return pick_tiles([grads[m] for m in range(n_mats)], parts, ids, counts, rows, lo, hi, size_b)

    def flat(value):
        return value.reshape((-1, size_b, size_b))

    def summed(mine, *got):
        return (flat(mine).astype(f32) + jnp.concatenate(got, axis=0).astype(f32)).astype(bf16)

    full_rows = theirs_rows + [mine_rows]
    grads[0] = dot_tn(inner_low, d_mlp_low).astype(bf16)
    if fast:
        out_a, out_b, mine_0 = cut_out(edge_b, count, 1, full_rows)
        got_0a = links.swap_x(flat(out_a))
        got_0b = links.swap_x(after(flat(out_b), got_0a))
        d_mlp_low = after(d_mlp_low, out_a)
    d_inner = dot_nt(d_mlp_low, w_down)
    d_gate = (d_inner * up_act * sig_gate * (1.0 + gate_act * (1.0 - sig_gate))).astype(bf16)
    d_up = (d_inner * silu_act).astype(bf16)
    if fast:
        d_up, d_gate = lax.optimization_barrier((d_up, d_gate, got_0a))[:2]
    grads[1] = dot_tn(hidden_low, d_up).astype(bf16)
    if fast:
        out_a, out_b, mine_1 = cut_out(edge_b1, edge_b, 2, full_rows)
        total_0 = links.reduce_z(summed(mine_0, got_0a, after(got_0b, out_a)))
        got_1a = links.swap_x(after(flat(out_a), got_0b))
        got_1b = links.swap_x(after(flat(out_b), got_1a))
        d_gate = after(d_gate, out_a, got_0b)
    grads[2] = dot_tn(hidden_low, d_gate).astype(bf16)
    d_up_in = after(d_up, grads[2])
    back_part = (dot_nt(d_gate, w_gate) + dot_nt(d_up_in, w_up)).astype(bf16)
    if fast:
        back_part = after(back_part, got_1a)
    sends = {}
    both_x = [theirs_rows[0] + theirs_rows[1], mine_rows]

    def while_reducing(both):
        grads[2] = after(grads[2], both)
        sends["2a"] = cut_out(edge_m, edge_b1, 3, both_x)
        sends["2b"] = cut_out(edge_a, edge_m, 3, both_x)
        return (sends["2b"][0],)

    def while_gathering(own):
        sum_1 = summed(mine_1, got_1a, after(got_1b, own))
        sends["outs"] = renew(after(total_0, sum_1), perm, edge_b, held, None)
        sends["1"] = links.reduce_z(sum_1)
        return (sum_1, sends["outs"][0])

    d_hidden = grad_rows + links.reduce_rows(back_part, while_reducing if fast else None)
    if fast:
        got_2a = links.swap_x(after(flat(sends["2a"][0]), got_1a))
        got_2b = links.swap_x(after(flat(sends["2b"][0]), got_2a))
    scaled_a = gain_full[2] * d_hidden
    d_branch = rms_a * scaled_a - branch * rms_a**3 * jnp.mean(scaled_a * branch, axis=-1, keepdims=True)
    d_branch_low = links.gather_rows(d_branch.astype(bf16), while_gathering if fast else None)
    d_attn = dot_nt(d_branch_low, w_o).astype(bf16)
    if fast:
        sum_2a = summed(sends["2a"][1], after(got_2a, d_attn))
        total_2a = links.reduce_z(sum_2a)
        d_attn = after(d_attn, sum_2a)
        total_1, outs = sends["1"], sends["outs"]
    d_qn, d_kn, d_values = attention_back(q_low, k_low, v_low, d_attn, cos_t, sin_t, lengths)
    scaled_q = gain_local[0] * d_qn
    scaled_k = gain_local[1] * d_kn
    gain_m_all = jnp.sum(grad_rows * mlp_rows * rms_m, axis=0)
    gain_a_all = jnp.sum(d_hidden * branch * rms_a, axis=0)
    sums = lax.psum(
        jnp.concatenate(
            [
                jnp.sum(scaled_q * queries, axis=-1),
                jnp.sum(scaled_k * keys_raw, axis=-1),
                gain_a_all,
                gain_m_all,
            ]
        ),
        "tensor",
    )
    stat_q, stat_k = sums[:slots], sums[slots : 2 * slots]
    gain_a_all, gain_m_all = sums[2 * slots : 2 * slots + width_d], sums[2 * slots + width_d :]
    d_queries = scale_q * scaled_q - queries * scale_q**3 * (stat_q / width_d)[:, None]
    d_keys = scale_k * scaled_k - keys_raw * scale_k**3 * (stat_k / width_d)[:, None]
    d_qkv = jnp.concatenate([d_queries.astype(bf16), d_keys.astype(bf16), d_values], axis=1)
    grads[4] = dot_tn(tok_full, d_qkv).astype(bf16)
    grads[3] = dot_tn(attn_low, d_branch_low).astype(bf16)
    if not fast:
        totals = []
        for lo, hi in ((edge_b, count), (edge_b1, edge_b), (edge_m, edge_b1), (edge_a, edge_m)):
            out_a, out_b, mine_n = cut_out(lo, hi, 5, full_rows)
            got_2a, got_2b = links.swap_x(flat(out_a)), links.swap_x(flat(out_b))
            totals.append(links.reduce_z(summed(mine_n, got_2a, got_2b)))
        total_0, total_1, total_2a, total_2b = totals
        outs = renew(total_0, perm, edge_b, held, None)

    mid = edge_a // 4 * 2
    turns = list(range(1, links.nz)) + [0]
    first_cut = cut_out(0, edge_a, 5, [[2 * turns[0] + 1], [2 * turns[0]]])
    grads[4] = after(grads[4], first_cut[0])
    rest = cut_out(0, edge_a, 5, [[2 * r + 1] for r in turns[1:]] + [[2 * r for r in turns[1:]]])
    to_send = [first_cut[0][0]] + [rest[k][0] for k in range(links.nz - 1)]
    to_keep = [first_cut[1][0]] + [rest[-1][k] for k in range(links.nz - 1)]
    pins = (rest[0],)
    late = [(edge_b1, total_1), (edge_m, total_2a), (edge_a, total_2b)] if not fast else []
    if fast:
        sum_2b = summed(sends["2b"][1], after(got_2b, rest[0]))
        total_2b = links.reduce_z(sum_2b)
        pins = (rest[0], sum_2b)
        late = [(edge_b1, total_1), (edge_m, total_2a), (edge_a, total_2b)]

    def joined(kept, got, ring):
        total = kept.astype(f32) + got.astype(f32)
        if ring is not None:
            total = total + ring.astype(f32)
        return total.astype(bf16)

    x_done = [got_2a, got_2b]
    ring = None
    for event in range(links.nz - 2):
        got = links.swap_x(after(to_send[event], x_done[-2]))
        x_done.append(got)
        total = joined(to_keep[event], after(got, *pins), ring)
        ring = links.ring(total)
        if event == 0:
            input_part = dot_nt(after(d_qkv, total), w_qkv).astype(bf16)
            pins = (input_part,)
        elif late:
            lo, ready = late.pop(0)
            outs = renew(after(ready, total), perm, lo, held, outs)
            pins = (outs[0],)
    halves = ((0, mid), (mid, edge_a))
    last_rings = []
    for lo, hi in halves:
        got = links.swap_x(after(to_send[-2][lo:hi], x_done[-2]))
        x_done.append(got)
        total = joined(to_keep[-2][lo:hi], after(got, *pins), ring[lo:hi])
        last_rings.append(links.ring(total))
        pins = ()
        if late:
            at, ready = late.pop(0)
            outs = renew(after(ready, total), perm, at, held, outs)
            pins = (outs[0],)
    gain_start = total
    for (lo, hi), ring in zip(halves, last_rings):
        got = links.swap_x(after(to_send[-1][lo:hi], x_done[-2]))
        x_done.append(got)
        total = joined(to_keep[-1][lo:hi], after(got, *pins), ring)
        pins = ()
        outs = renew(total, perm, lo, held, outs)

    input_rows = links.reduce_rows(input_part)
    token_grads = links.rows_to_cols((input_rows + d_hidden).astype(bf16))
    block_out = links.rows_to_cols(after(result, x_done[3]).astype(bf16))

    gain_terms = jnp.stack(
        [
            jnp.sum(d_qn * queries * scale_q, axis=0),
            jnp.sum(d_kn * keys_raw * scale_k, axis=0),
            lax.dynamic_slice_in_dim(gain_a_all, links.t * width_local, width_local, 0),
            lax.dynamic_slice_in_dim(gain_m_all, links.t * width_local, width_local, 0),
        ]
    )
    gain_terms = after(gain_terms, gain_start)
    gain_part = gain_terms + links.swap_x(gain_terms)
    gain_grads = gain_part
    for r in range(1, links.nz):
        gain_part = links.ring(gain_part)
        gain_grads = gain_grads + gain_part
    gain_stats_new = DECAY * gain_stats + (1.0 - DECAY) * gain_grads * gain_grads
    gains_new = gains - GAIN_RATE * gain_grads * gain_roots

    block_grads, left_new, right_new, master_new = (out[None] for out in outs)
    return (
        block_out,
        token_grads,
        block_grads,
        left_new,
        right_new,
        master_new,
        gain_grads,
        gain_stats_new,
        gains_new,
    )


def tile_edges(width_local, width_d, hidden_local, size_b):
    cols_w, cols_h, cols_d = width_local // size_b, hidden_local // size_b, width_d // size_b
    sizes = [cols_d * cols_w] * 4 + [cols_d * cols_h] * 3
    return [sum(sizes[:i]) for i in range(8)], cols_w, cols_h, cols_d


def cut_points(count):
    def at(part):
        return count * part // 128 // 2 * 2

    a, b1, b = at(48), at(84), at(112)
    return {"a": a, "b1": b1, "b": b, "end": count}


def body(
    tokens,
    cotangent,
    lengths,
    gains,
    gain_stats,
    gain_roots,
    master,
    block_order,
    left_stats,
    right_stats,
    left_roots,
    right_roots,
):
    links = Links()
    count, size_b = master.shape[1], master.shape[-1]
    cuts = cut_points(count)
    order = block_order[0].reshape(links.n_dp, count)
    rank = jnp.sum(order[:, None, :] < order[:, :, None], axis=2, dtype=jnp.int32)
    hit = rank[:, None, :] == jnp.arange(count)[None, :, None]
    sorted_ids = jnp.sum(jnp.where(hit, order[:, None, :], 0), axis=2, dtype=jnp.int32)
    rank_own = lax.dynamic_index_in_dim(rank, links.d, 0, False)
    perm = jnp.sum(
        jnp.where(rank_own[None, :] == jnp.arange(count)[:, None], jnp.arange(count)[None, :], 0),
        axis=1,
        dtype=jnp.int32,
    )
    width_local = tokens.shape[1]
    edges = tile_edges(width_local, width_local * links.n_t, FF // links.n_t, size_b)[0]
    counts = jnp.sum(order[:, None, :] < jnp.asarray(edges, jnp.int32)[None, :, None], axis=2, dtype=jnp.int32)
    fits = jnp.all((counts[:, 4] <= cuts["a"]) & (counts[:, 5] <= cuts["b1"]) & (counts[:, 6] <= cuts["b"]))

    table = jnp.concatenate([sorted_ids, counts], axis=1).reshape(links.nz, 2, count + 8)
    table = jnp.where(links.x == 0, table, table[:, ::-1])
    twice = jnp.concatenate([table, table], axis=0)
    ring = lax.dynamic_slice_in_dim(twice, links.z, links.nz, 0)
    table = jnp.concatenate([ring, table], axis=0).reshape(2 * links.n_dp, count + 8)
    tables = (table[:, :count], table[:, count:])
    flag = jnp.broadcast_to(jnp.where(fits, 1.0, 0.0), (1, tokens.shape[1]))
    shared = lax.all_gather(
        jnp.concatenate([gains, flag], axis=0).astype(bf16), "tensor", axis=1, tiled=True
    ).astype(f32)
    gain_full, all_fit = shared[:4], jnp.min(shared[4]) > 0.5
    args = (tokens, cotangent, lengths, gains, gain_stats, gain_roots)
    args = args + (master[0], left_stats[0], right_stats[0], left_roots[0], right_roots[0])

    def run(fast):
        return lambda *rest: core(fast, cuts, links, tables, perm, gain_full, rest)

    if MODE == "fast":
        return run(True)(*args)
    return lax.cond(all_fit, run(True), run(False), *args)


MODE = "cond"


def solution(mesh):
    placed = (
        P("dp", "tensor"),
        P("dp", "tensor"),
        P("dp"),
        P(None, "tensor"),
        P(None, "tensor"),
        P(None, "tensor"),
        P("tensor", "dp", None, None),
        P("tensor", None),
        P("tensor", "dp", None, None),
        P("tensor", "dp", None, None),
        P("tensor", "dp", None, None),
        P("tensor", "dp", None, None),
    )
    return jax.shard_map(
        body,
        mesh=mesh,
        in_specs=placed,
        out_specs=(
            P("dp", "tensor"),
            P("dp", "tensor"),
            P("tensor", "dp", None, None),
            P("tensor", "dp", None, None),
            P("tensor", "dp", None, None),
            P("tensor", "dp", None, None),
            P(None, "tensor"),
            P(None, "tensor"),
            P(None, "tensor"),
        ),
        check_vma=False,
    )
```

```python
import jax
import jax.numpy as jnp
import numpy as np
from jax import lax
from jax.experimental import pallas as pl
from jax.experimental.pallas import tpu as pltpu
from jax.sharding import PartitionSpec as P

HEADS = 16
HD = 128
FF = 8192
EPSILON = 1e-06
THETA = 500000.0
DECAY = 0.5
LEARN_RATE = 0.25
GAIN_RATE = 0.2
NEG = -1e30
MIB = 1024 * 1024
f32 = jnp.float32
bf16 = jnp.bfloat16


def after(value, *others):
    return lax.optimization_barrier((value,) + others)[0]


class Links:
    def __init__(self):
        self.n_dp = lax.axis_size("dp")
        self.n_t = lax.axis_size("tensor")
        self.nz = self.n_dp // 2
        self.ny = self.n_t // 2
        self.d = lax.axis_index("dp")
        self.z, self.x = self.d // 2, self.d % 2
        self.t = lax.axis_index("tensor")
        self.y, self.c = self.t // 2, self.t % 2
        self.z_groups = [[2 * z + x for z in range(self.nz)] for x in range(2)]

    def ring(self, value):
        pairs = [(2 * z + x, 2 * ((z - 1) % self.nz) + x) for z in range(self.nz) for x in range(2)]
        return lax.ppermute(value, "dp", pairs)

    def gather_z(self, value):
        return lax.all_gather(value, "dp", axis=0, tiled=True, axis_index_groups=self.z_groups)

    def reduce_z(self, value):
        return lax.psum_scatter(
            value, "dp", scatter_dimension=0, tiled=True, axis_index_groups=self.z_groups
        )

    def swap_x(self, value):
        return lax.ppermute(value, "dp", [(i, i ^ 1) for i in range(self.n_dp)])

    def swap_core(self, value):
        return lax.ppermute(value, "tensor", [(i, i ^ 1) for i in range(self.n_t)])

    def shift_y(self, value, step):
        pairs = [(i, 2 * ((i // 2 + step) % self.ny) + i % 2) for i in range(self.n_t)]
        return lax.ppermute(value, "tensor", pairs)

    def shift_t(self, value, step):
        return lax.ppermute(value, "tensor", [(i, (i + step) % self.n_t) for i in range(self.n_t)])

    def gather_rows(self, own, meanwhile=None):
        pieces = [(self.y, own)]
        for step in range(1, self.ny):
            got = self.shift_y(own, step)
            if meanwhile is not None and step == 1:
                got = after(got, *meanwhile(own))
            pieces.append(((self.y + self.ny - step) % self.ny, got))
        parts, places = [], []
        for row_y, piece in pieces:
            parts += [piece, self.swap_core(piece)]
            places += [2 * row_y + self.c, 2 * row_y + 1 - self.c]
        return stack_rows(parts, jnp.stack(places))

    def reduce_rows(self, part, meanwhile=None):
        rows = part.shape[0] // self.n_t
        cut = part.reshape((self.ny, 2, rows, part.shape[1]))
        got = self.swap_core(lax.dynamic_index_in_dim(cut, 1 - self.c, 1, False))
        kept = lax.dynamic_index_in_dim(cut, self.c, 1, False)
        both = (kept.astype(f32) + got.astype(f32)).astype(bf16)
        total = lax.dynamic_index_in_dim(both, self.y, 0, False).astype(f32)
        for step in range(1, self.ny):
            piece = lax.dynamic_index_in_dim(both, (self.y + step) % self.ny, 0, False)
            got = self.shift_y(piece, step)
            if meanwhile is not None and step == 1:
                got = after(got, *meanwhile(both))
            total = total + got.astype(f32)
        return total

    def rows_to_cols(self, own):
        rows, width = own.shape[0], own.shape[1] // self.n_t
        full = jnp.zeros((rows * self.n_t, width), own.dtype)
        for step in range(self.n_t):
            piece = lax.dynamic_slice_in_dim(own, ((self.t + step) % self.n_t) * width, width, 1)
            if step:
                piece = self.shift_t(piece, step)
            row0 = ((self.t + self.n_t - step) % self.n_t) * rows
            full = lax.dynamic_update_slice_in_dim(full, piece, row0, 0)
        return full


def fit(count, most=8):
    return next(step for step in (8, 4, 2, 1) if step <= most and count % step == 0)


def stack_rows(parts, places):
    rows, cols = parts[0].shape
    n = len(parts)

    def kernel(places_ref, *refs):
        out, sem = refs[n], refs[n + 1]
        copies = []
        for i in range(n):
            start = pl.multiple_of(places_ref[i] * rows, rows)
            copies.append(pltpu.make_async_copy(refs[i], out.at[pl.ds(start, rows), :], sem.at[i]))
            copies[-1].start()
        for copy in copies:
            copy.wait()

    return pl.pallas_call(
        kernel,
        grid_spec=pltpu.PrefetchScalarGridSpec(
            num_scalar_prefetch=1,
            grid=(1,),
            in_specs=[pl.BlockSpec(memory_space=pl.ANY)] * n,
            out_specs=pl.BlockSpec(memory_space=pltpu.VMEM),
            scratch_shapes=[pltpu.SemaphoreType.DMA((n,))],
        ),
        out_shape=jax.ShapeDtypeStruct((n * rows, cols), parts[0].dtype),
        compiler_params=pltpu.CompilerParams(vmem_limit_bytes=32 * MIB),
        name="stack_rows",
    )(places, *parts)


def sorted_tiles(master, perm, lo, hi):
    size_b = master.shape[-1]
    step = fit(hi - lo)

    def kernel(perm_ref, *refs):
        for j in range(step):
            refs[step][j] = refs[j][0].astype(bf16)

    def spec(j):
        return pl.BlockSpec((1, size_b, size_b), lambda i, p: (p[lo + step * i + j], 0, 0))

    return pl.pallas_call(
        kernel,
        grid_spec=pltpu.PrefetchScalarGridSpec(
            num_scalar_prefetch=1,
            grid=((hi - lo) // step,),
            in_specs=[spec(j) for j in range(step)],
            out_specs=pl.BlockSpec((step, size_b, size_b), lambda i, p: (i, 0, 0)),
        ),
        out_shape=jax.ShapeDtypeStruct((hi - lo, size_b, size_b), bf16),
        name="sorted_tiles",
    )(perm, *([master] * step))


def place_tiles(sources, parts, shapes, ids, counts, size_b):
    arrays = []
    for source in sources:
        if not any(source[0] is array for array in arrays):
            arrays.append(source[0])
    places = [next(i for i, array in enumerate(arrays) if array is source[0]) for source in sources]
    n_src, n_out = len(arrays), len(shapes)

    def kernel(ids_ref, counts_ref, *refs):
        outs, sem = refs[n_src : n_src + n_out], refs[-1]
        for m, edge, base, cols, off in parts:
            for s, (_, at, row, lo, hi) in zip(places, sources):

                def step(k, carry, s=s, m=m, base=base, cols=cols, off=off, row=row, skip=lo - at):
                    tile = ids_ref[row, k] - base
                    r = tile >> (cols.bit_length() - 1)
                    c = (tile & (cols - 1)) + off
                    pltpu.make_async_copy(
                        refs[s].at[k - skip],
                        outs[m].at[
                            pl.ds(pl.multiple_of(r * size_b, size_b), size_b),
                            pl.ds(pl.multiple_of(c * size_b, size_b), size_b),
                        ],
                        sem,
                    ).start()
                    return carry

                first = jnp.maximum(counts_ref[row, edge], lo)
                last = jnp.minimum(counts_ref[row, edge + 1], hi)
                lax.fori_loop(first, last, step, 0)
        for out in outs:
            pltpu.make_async_copy(out, out, sem).wait()

    return pl.pallas_call(
        kernel,
        grid_spec=pltpu.PrefetchScalarGridSpec(
            num_scalar_prefetch=2,
            grid=(1,),
            in_specs=[pl.BlockSpec(memory_space=pl.ANY)] * n_src,
            out_specs=[pl.BlockSpec(memory_space=pltpu.VMEM)] * n_out,
            scratch_shapes=[pltpu.SemaphoreType.DMA],
        ),
        out_shape=[jax.ShapeDtypeStruct(shape, bf16) for shape in shapes],
        compiler_params=pltpu.CompilerParams(vmem_limit_bytes=60 * MIB),
        name="place_tiles",
    )(ids, counts, *arrays)


def pick_tiles(matrices, parts, ids, counts, rows, lo, hi, size_b, extra=None):
    n_mat, n_out = len(matrices), len(rows)
    more = [] if extra is None else [extra]
    n_src = n_mat + len(more)

    def kernel(ids_ref, counts_ref, *refs):
        outs, sem = refs[n_src : n_src + n_out], refs[-1]
        for m, edge, base, cols, off in parts:
            for i, group in enumerate(rows):
                for j, row in enumerate(group):

                    def step(k, carry, i=i, j=j, row=row, m=m, base=base, cols=cols, off=off):
                        tile = ids_ref[row, k] - base
                        r = tile >> (cols.bit_length() - 1)
                        c = (tile & (cols - 1)) + off
                        pltpu.make_async_copy(
                            refs[m].at[
                                pl.ds(pl.multiple_of(r * size_b, size_b), size_b),
                                pl.ds(pl.multiple_of(c * size_b, size_b), size_b),
                            ],
                            outs[i].at[j, k - lo],
                            sem,
                        ).start()
                        return carry

                    first = jnp.maximum(counts_ref[row, edge], lo)
                    last = jnp.minimum(counts_ref[row, edge + 1], hi)
                    lax.fori_loop(first, last, step, 0)
        if more:
            for i, group in enumerate(rows):
                for j in range(len(group)):
                    pltpu.make_async_copy(refs[n_mat], outs[i].at[j, hi - lo], sem).start()
        for out in outs:
            pltpu.make_async_copy(out, out, sem).wait()

    return pl.pallas_call(
        kernel,
        grid_spec=pltpu.PrefetchScalarGridSpec(
            num_scalar_prefetch=2,
            grid=(1,),
            in_specs=[pl.BlockSpec(memory_space=pl.ANY)] * n_src,
            out_specs=[pl.BlockSpec(memory_space=pltpu.VMEM)] * n_out,
            scratch_shapes=[pltpu.SemaphoreType.DMA],
        ),
        out_shape=[
            jax.ShapeDtypeStruct((len(group), hi - lo + len(more), size_b, size_b), bf16) for group in rows
        ],
        compiler_params=pltpu.CompilerParams(vmem_limit_bytes=60 * MIB),
        name="pick_tiles",
    )(ids, counts, *matrices, *more)


def dot_nt(a, b):
    return lax.dot_general(a, b, (((1,), (1,)), ((), ())), preferred_element_type=f32)


def dot_tn(a, b):
    return lax.dot_general(a, b, (((0,), (0,)), ((), ())), preferred_element_type=f32)


def dot_nn(a, b):
    return lax.dot_general(a, b, (((1,), (0,)), ((), ())), preferred_element_type=f32)


def kept(shape):
    return pl.BlockSpec(shape, lambda i: (0,) * len(shape), pipeline_mode=pl.Buffered(1))


ROOMY = pltpu.CompilerParams(vmem_limit_bytes=52 * MIB)


def product_tn(a, b):
    (rows, m), n = a.shape, b.shape[1]
    step = min(512, m)

    def kernel(a_ref, b_ref, out_ref):
        out_ref[...] = dot_tn(a_ref[...], b_ref[...]).astype(bf16)

    return pl.pallas_call(
        kernel,
        grid=(m // step,),
        in_specs=[pl.BlockSpec((rows, step), lambda i: (0, i)), kept((rows, n))],
        out_specs=pl.BlockSpec((step, n), lambda i: (i, 0)),
        out_shape=jax.ShapeDtypeStruct((m, n), bf16),
        compiler_params=ROOMY,
        name="product_tn",
    )(a, b)


def product_nt(*pairs):
    count, rows, n = len(pairs), pairs[0][0].shape[0], pairs[0][1].shape[0]
    step = min(256, n)

    def kernel(*refs):
        total = dot_nt(refs[0][...], refs[count][...])
        for i in range(1, count):
            total = total + dot_nt(refs[i][...], refs[count + i][...])
        refs[-1][...] = total.astype(bf16)

    return pl.pallas_call(
        kernel,
        grid=(n // step,),
        in_specs=[kept(a.shape) for a, _ in pairs]
        + [pl.BlockSpec((step, b.shape[1]), lambda i: (i, 0)) for _, b in pairs],
        out_specs=pl.BlockSpec((rows, step), lambda i: (0, i)),
        out_shape=jax.ShapeDtypeStruct((rows, n), bf16),
        compiler_params=ROOMY,
        name="product_nt",
    )(*[a for a, _ in pairs], *[b for _, b in pairs])


def inner_back(d_mlp, w_down, gate_act, up_act):
    rows, hidden = gate_act.shape
    step = min(512, hidden)

    def kernel(d_ref, w_ref, gate_ref, up_ref, d_gate_ref, d_up_ref):
        d_inner = dot_nt(d_ref[...], w_ref[...])
        gate = gate_ref[...]
        sig = jax.nn.sigmoid(gate)
        d_gate_ref[...] = (d_inner * up_ref[...] * sig * (1.0 + gate * (1.0 - sig))).astype(bf16)
        d_up_ref[...] = (d_inner * (gate * sig)).astype(bf16)

    strip = pl.BlockSpec((rows, step), lambda i: (0, i))
    return pl.pallas_call(
        kernel,
        grid=(hidden // step,),
        in_specs=[kept(d_mlp.shape), pl.BlockSpec((step, w_down.shape[1]), lambda i: (i, 0)), strip, strip],
        out_specs=[strip, strip],
        out_shape=[jax.ShapeDtypeStruct((rows, hidden), bf16)] * 2,
        compiler_params=ROOMY,
        name="inner_back",
    )(d_mlp, w_down, gate_act, up_act)


def softmax_block(q_block, k_head, first, length):
    keys = k_head.shape[0]
    scores = dot_nt(q_block, k_head) * (HD**-0.5)
    rows = first + lax.broadcasted_iota(jnp.int32, scores.shape, 0)
    cols = lax.broadcasted_iota(jnp.int32, scores.shape, 1)
    scores = jnp.where((cols <= rows) & (cols < length), scores, NEG)
    probs = jnp.exp(scores - jnp.max(scores, axis=-1, keepdims=True))
    return probs / jnp.sum(probs, axis=-1, keepdims=True)


def attention(raw, scale_q, scale_k, gains, cos_t, sin_t, lengths):
    slots, width = raw.shape[0], raw.shape[1] // 3
    heads = width // HD
    block = min(256, slots)

    def kernel(len_ref, q_ref, k_ref, v_ref, sq_ref, sk_ref, gain_ref, cos_ref, sin_ref, out_ref, ql_ref, kl_ref, vl_ref):
        def turned(ref, scale, row):
            val = ref[...] * scale[...] * gain_ref[row : row + 1, :]
            return (val * cos_ref[...] + pltpu.roll(val, HD // 2, 1) * sin_ref[...]).astype(bf16)

        ql_ref[...] = turned(q_ref, sq_ref, 0)
        kl_ref[...] = turned(k_ref, sk_ref, 1)
        vl_ref[...] = v_ref[...].astype(bf16)
        for first in range(0, slots, block):
            last = first + block
            probs = softmax_block(ql_ref[first:last, :], kl_ref[:last, :], first, len_ref[0])
            out_ref[first:last, :] = dot_nn(probs.astype(bf16), vl_ref[:last, :]).astype(bf16)

    def head_spec(part):
        return pl.BlockSpec((slots, HD), lambda h, n: (0, part * heads + h))

    whole = lambda shape: pl.BlockSpec(shape, lambda h, n: (0, 0))
    out_spec = pl.BlockSpec((slots, HD), lambda h, n: (0, h))
    return pl.pallas_call(
        kernel,
        grid_spec=pltpu.PrefetchScalarGridSpec(
            num_scalar_prefetch=1,
            grid=(heads,),
            in_specs=[head_spec(0), head_spec(1), head_spec(2), whole((slots, 1)), whole((slots, 1))]
            + [pl.BlockSpec((4, HD), lambda h, n: (0, h)), whole((slots, HD)), whole((slots, HD))],
            out_specs=[out_spec] * 4,
        ),
        out_shape=[jax.ShapeDtypeStruct((slots, width), bf16)] * 4,
        compiler_params=pltpu.CompilerParams(vmem_limit_bytes=48 * MIB),
        name="attention",
    )(lengths, raw, raw, raw, scale_q, scale_k, gains, cos_t, sin_t)


def attention_back(q_low, k_low, v_low, d_attn, cos_t, sin_t, lengths):
    slots, width = q_low.shape
    heads = width // HD
    block = min(256, slots)

    def kernel(len_ref, q_ref, k_ref, v_ref, do_ref, cos_ref, sin_ref, dq_ref, dk_ref, dv_ref, dk_acc, dv_acc):
        def turned_back(val, rows):
            return val * cos_ref[rows, :] - pltpu.roll(val, HD // 2, 1) * sin_ref[rows, :]

        dk_acc[...] = jnp.zeros_like(dk_acc)
        dv_acc[...] = jnp.zeros_like(dv_acc)
        for first in range(0, slots, block):
            last = first + block
            rows, keys = slice(first, last), slice(0, last)
            probs = softmax_block(q_ref[rows, :], k_ref[keys, :], first, len_ref[0])
            d_out = do_ref[rows, :]
            d_probs = dot_nt(d_out, v_ref[keys, :])
            delta = jnp.sum(probs * d_probs, axis=-1, keepdims=True)
            d_scores = (probs * (d_probs - delta)).astype(bf16)
            dq_ref[rows, :] = turned_back(dot_nn(d_scores, k_ref[keys, :]) * (HD**-0.5), rows)
            dk_acc[keys, :] += dot_tn(d_scores, q_ref[rows, :])
            dv_acc[keys, :] += dot_tn(probs.astype(bf16), d_out)
        dk_ref[...] = turned_back(dk_acc[...] * (HD**-0.5), slice(0, slots))
        dv_ref[...] = dv_acc[...].astype(bf16)

    spec = pl.BlockSpec((slots, HD), lambda h, n: (0, h))
    whole = pl.BlockSpec((slots, HD), lambda h, n: (0, 0))
    return pl.pallas_call(
        kernel,
        grid_spec=pltpu.PrefetchScalarGridSpec(
            num_scalar_prefetch=1,
            grid=(heads,),
            in_specs=[spec] * 4 + [whole] * 2,
            out_specs=[spec] * 3,
            scratch_shapes=[pltpu.VMEM((slots, HD), f32)] * 2,
        ),
        out_shape=[
            jax.ShapeDtypeStruct((slots, width), f32),
            jax.ShapeDtypeStruct((slots, width), f32),
            jax.ShapeDtypeStruct((slots, width), bf16),
        ],
        compiler_params=pltpu.CompilerParams(vmem_limit_bytes=48 * MIB),
        name="attention_back",
    )(lengths, q_low, k_low, v_low, d_attn, cos_t, sin_t)


def renew(grads, perm, lo, held, outs, fetched=None):
    count, size_b = grads.shape[0], grads.shape[-1]
    n_old = 0 if outs is None else len(outs)
    batch = fit(count)
    steps = count // batch

    n_in = 5 * batch if fetched is None else 1

    def kernel(perm_ref, g_ref, *refs):
        outs_ref = refs[n_in + n_old : n_in + n_old + 4]
        held_ref, sems = refs[-2:]
        i = pl.program_id(0)
        side = i % 2

        def drain(which):
            pltpu.make_async_copy(held_ref.at[which], held_ref.at[which], sems.at[which]).wait()

        @pl.when(i >= 2)
        def _():
            drain(side)

        for j in range(batch):
            if fetched is None:
                tiles = [refs[a * batch + j][0] for a in range(5)]
            else:
                tiles = [refs[0][j, a] for a in range(5)]
            master, left_s, right_s, left_r, right_r = tiles
            g = g_ref[j]
            held_ref[side, 0, j] = g.astype(f32)
            held_ref[side, 1, j] = DECAY * left_s + (1.0 - DECAY) * dot_nt(g, g)
            held_ref[side, 2, j] = DECAY * right_s + (1.0 - DECAY) * dot_tn(g, g)
            left = dot_nn(left_r.astype(bf16), g).astype(bf16)
            held_ref[side, 3, j] = master - LEARN_RATE * dot_nn(left, right_r.astype(bf16))
        for j in range(batch):
            slot = perm_ref[lo + batch * i + j]
            for a in range(4):
                pltpu.make_async_copy(held_ref.at[side, a, j], outs_ref[a].at[slot], sems.at[side]).start()

        @pl.when(i == steps - 1)
        def _():
            drain(side)
            if steps > 1:
                drain(1 - side)

    def spec(j):
        return pl.BlockSpec((1, size_b, size_b), lambda i, p: (p[lo + batch * i + j], 0, 0))

    return pl.pallas_call(
        kernel,
        grid_spec=pltpu.PrefetchScalarGridSpec(
            num_scalar_prefetch=1,
            grid=(steps,),
            in_specs=[pl.BlockSpec((batch, size_b, size_b), lambda i, p: (i, 0, 0))]
            + (
                [spec(j) for _ in range(5) for j in range(batch)]
                if fetched is None
                else [pl.BlockSpec((batch, 5, size_b, size_b), lambda i, p: (lo // batch + i, 0, 0, 0))]
            )
            + [pl.BlockSpec(memory_space=pl.ANY)] * n_old,
            out_specs=[pl.BlockSpec(memory_space=pl.ANY)] * 4,
            scratch_shapes=[
                pltpu.VMEM((2, 4, batch, size_b, size_b), f32),
                pltpu.SemaphoreType.DMA((2,)),
            ],
        ),
        out_shape=[jax.ShapeDtypeStruct(held[0].shape, f32)] * 4,
        input_output_aliases={2 + n_in + i: i for i in range(n_old)},
        compiler_params=pltpu.CompilerParams(vmem_limit_bytes=40 * MIB),
        name="renew",
    )(perm, grads, *([array for array in held for _ in range(batch)] if fetched is None else [fetched]), *(outs or ()))


def fetch(perm, count, held):
    size_b = held[0].shape[-1]

    def kernel(perm_ref, *refs):
        out, sem = refs[-2:]

        def step(k, carry):
            slot = perm_ref[k]
            for a in range(5):
                pltpu.make_async_copy(refs[a].at[slot], out.at[k, a], sem).start()
            return carry

        lax.fori_loop(0, count, step, 0)
        pltpu.make_async_copy(out, out, sem).wait()

    return pl.pallas_call(
        kernel,
        grid_spec=pltpu.PrefetchScalarGridSpec(
            num_scalar_prefetch=1,
            grid=(1,),
            in_specs=[pl.BlockSpec(memory_space=pl.ANY)] * 5,
            out_specs=pl.BlockSpec(memory_space=pltpu.VMEM),
            scratch_shapes=[pltpu.SemaphoreType.DMA],
        ),
        out_shape=jax.ShapeDtypeStruct((count, 5, size_b, size_b), f32),
        compiler_params=pltpu.CompilerParams(vmem_limit_bytes=40 * MIB),
        name="fetch",
    )(perm, *held)


def rope_tables(seq_len):
    half = HD // 2
    freqs = THETA ** (-(2.0 * jnp.arange(half, dtype=f32)) / HD)
    angles = jnp.arange(seq_len, dtype=f32)[:, None] * freqs[None, :]
    cos_t, sin_t = jnp.cos(angles), jnp.sin(angles)
    return jnp.concatenate([cos_t, cos_t], 1), jnp.concatenate([-sin_t, sin_t], 1)


def gather_front(links, cuts, tokens, master, perm):
    edge_a, edge_b1, edge_b, count = cuts["a"], cuts["b1"], cuts["b"], cuts["end"]
    own_a = sorted_tiles(master, perm, 0, edge_a)
    later = after(perm, own_a)
    owns = [sorted_tiles(master, later, lo, hi) for lo, hi in ((edge_a, edge_b1), (edge_b1, edge_b), (edge_b, count))]
    tok_full = lax.all_gather(tokens, "tensor", axis=1, tiled=True)
    return owns, own_a, links.swap_x(own_a), links.ring(own_a), tok_full


def core(fast, cuts, links, tables, perm, gain_full, front, args):
    tokens, cotangent, lengths, gains, gain_stats, gain_roots = args[:6]
    master, left_stats, right_stats, left_roots, right_roots = args[6:]
    ids, counts = tables
    size_b = master.shape[-1]
    slots, width_local = tokens.shape
    n_t = links.n_t
    width_d = width_local * n_t
    hidden_local = FF // n_t
    count = master.shape[0]

    edges, cols_w, cols_h, cols_d = tile_edges(width_local, width_d, hidden_local, size_b)
    qkv_parts = [(i, edges[i], cols_w, i * cols_w) for i in range(3)]
    o_part, gate_part, up_part, down_part = (
        (3 + i, edges[3 + i], cols, 0) for i, cols in enumerate((cols_d, cols_h, cols_h, cols_d))
    )

    edge_a, edge_b1, edge_b, count = cuts["a"], cuts["b1"], cuts["b"], cuts["end"]
    owns, own_a, their_a, next_a, tok_full = front
    mine, theirs = [own_a, next_a], [their_a]
    for r in range(2, links.nz):
        mine.append(links.ring(after(mine[-1], theirs[r - 2])))
        theirs.append(links.swap_x(after(mine[r - 1], theirs[-1])))
    theirs.append(links.swap_x(after(mine[-1], theirs[-1])))
    own_b1 = links.swap_x(after(owns[0], theirs[-1]))
    own_c = links.swap_x(after(owns[2], own_b1))
    own_b2 = links.swap_x(after(owns[1], own_b1))
    cot_full = lax.all_gather(cotangent, "tensor", axis=1, tiled=True)
    sources_a = []
    for r in range(links.nz):
        sources_a.append((mine[r], 0, 2 * r, 0, edge_a))
        sources_a.append((theirs[r], 0, 2 * r + 1, 0, edge_a))

    def matrices(sources, groups, shapes):
        return place_tiles(sources, [(m,) + part for m, part in groups], shapes, ids, counts, size_b)

    def others(gathered, n):
        return [
            lax.dynamic_slice_in_dim(gathered, ((links.z + r) % links.nz) * n, n, 0) for r in range(1, links.nz)
        ]

    def send_others(pieces, last):
        sent = []
        for piece in pieces:
            last = links.swap_x(after(piece, last))
            sent.append(last)
        return sent

    def all_sources(lo, hi, gathered, own_x, rest_x):
        n = hi - lo
        found = [(gathered, z * n, links.n_dp + 2 * z, lo, hi) for z in range(links.nz)]
        found.append((own_x, 0, 1, lo, hi))
        return found + [(rest_x[r - 1], 0, 2 * r + 1, lo, hi) for r in range(1, links.nz)]

    n_b1, n_b2, n_c = edge_b1 - edge_a, edge_b - edge_b1, count - edge_b
    z_b1, z_b2, z_c = (
        links.gather_z(after(own, mine[-1], theirs[-2])) for own in (owns[0], owns[1], jnp.concatenate([owns[2], own_c], axis=0))
    )
    pieces_b1 = others(z_b1, n_b1)
    rest_b1 = send_others(pieces_b1, own_b2)
    rest_b2 = send_others(others(z_b2, n_b2), rest_b1[-1])
    sources_b1 = sources_a + all_sources(edge_a, edge_b1, z_b1, own_b1, rest_b1)
    sources_b2 = sources_b1 + all_sources(edge_b1, edge_b, z_b2, own_b2, rest_b2)
    sources_c = sources_b2 + [
        (z_c, (2 * z + xr) * n_c, links.n_dp + 2 * z + xr, edge_b, count) for z in range(links.nz) for xr in range(2)
    ]
    if not fast:
        sources_a = sources_b1 = sources_b2 = sources_c

    gain_local = gains.astype(bf16).astype(f32)
    length = lengths[0]
    cos_t, sin_t = rope_tables(slots)
    own_rows = slots // n_t
    row0 = links.t * own_rows
    tok_rows = lax.dynamic_slice_in_dim(tok_full, row0, own_rows, 0).astype(f32)
    live = (row0 + jnp.arange(own_rows) < length).astype(f32)[:, None]
    grad_rows = lax.dynamic_slice_in_dim(cot_full, row0, own_rows, 0).astype(f32) * live

    w_qkv, w_o = matrices(
        sources_a,
        [(0, part) for part in qkv_parts] + [(1, o_part)],
        [(width_d, 3 * width_local), (width_local, width_d)],
    )
    raw = after(dot_nn(tok_full, w_qkv), own_b1)
    queries, keys_raw = raw[:, :width_local], raw[:, width_local : 2 * width_local]
    squares = lax.psum(
        jnp.stack([jnp.sum(queries * queries, axis=-1), jnp.sum(keys_raw * keys_raw, axis=-1)]), "tensor"
    )
    scale_q = lax.rsqrt(squares[0] / width_d + EPSILON)[:, None]
    scale_k = lax.rsqrt(squares[1] / width_d + EPSILON)[:, None]
    attn_low, q_low, k_low, v_low = attention(raw, scale_q, scale_k, gain_local, cos_t, sin_t, lengths)
    branch = links.reduce_rows(dot_nn(after(attn_low, own_c, own_b2, pieces_b1[0]), w_o).astype(bf16))
    rms_a = lax.rsqrt(jnp.mean(branch * branch, axis=-1, keepdims=True) + EPSILON)
    hidden_rows = tok_rows + branch * rms_a * gain_full[2]
    hidden_low = links.gather_rows(hidden_rows.astype(bf16))
    hidden_low = after(hidden_low, rest_b1[0])

    (w_gate,) = matrices(sources_b1, [(0, gate_part)], [(width_d, hidden_local)])
    gate_act = dot_nn(hidden_low, w_gate)
    sig_gate = jax.nn.sigmoid(gate_act)
    silu_act = gate_act * sig_gate
    (w_down,) = matrices(sources_c, [(0, down_part)], [(hidden_local, width_d)])
    sources_b2 = [(after(sources_b2[0][0], w_down),) + sources_b2[0][1:]] + sources_b2[1:]
    (w_up,) = matrices(sources_b2, [(0, up_part)], [(width_d, hidden_local)])
    up_act = dot_nn(hidden_low, w_up)
    inner_low = (silu_act * up_act).astype(bf16)
    mlp_rows = links.reduce_rows(dot_nn(inner_low, w_down).astype(bf16))
    rms_m = lax.rsqrt(jnp.mean(mlp_rows * mlp_rows, axis=-1, keepdims=True) + EPSILON)
    result = hidden_rows + mlp_rows * rms_m * gain_full[3]
    scaled_m = gain_full[3] * grad_rows
    d_mlp = rms_m * scaled_m - mlp_rows * rms_m**3 * jnp.mean(scaled_m * mlp_rows, axis=-1, keepdims=True)
    d_mlp_low = links.gather_rows(d_mlp.astype(bf16))

    grads = {}
    grad_parts = [(0, down_part), (1, up_part), (2, gate_part), (3, o_part)] + [(4, p) for p in qkv_parts]
    held = (master, left_stats, right_stats, left_roots, right_roots)
    edge_m = (edge_a + edge_b1) // 4 * 2
    rows_x = [[links.n_dp + 2 * z + xr for z in range(links.nz)] for xr in (1, 0)]
    half_z = links.nz // 2
    rows_halves = [rows_x[0][:half_z], rows_x[0][half_z:], rows_x[1]]

    def cut_out(lo, hi, n_mats, rows, extra=None):
        parts = [(m,) + part for m, part in grad_parts if m < n_mats]
        return pick_tiles([grads[m] for m in range(n_mats)], parts, ids, counts, rows, lo, hi, size_b, extra)

    def flat(value):
        return value.reshape((-1, size_b, size_b))

    def summed(mine, *got):
        return (flat(mine).astype(f32) + jnp.concatenate(got, axis=0).astype(f32)).astype(bf16)

    grads[0] = product_tn(inner_low, d_mlp_low)
    if fast:
        out_0, mine_0 = cut_out(edge_b, count, 1, rows_x)
        got_0 = links.swap_x(flat(out_0))
        d_mlp_low = after(d_mlp_low, out_0)
    d_gate, d_up = inner_back(d_mlp_low, w_down, gate_act, up_act)
    grads[1] = product_tn(hidden_low, d_up)
    if fast:
        out_1a, out_1b, mine_1 = cut_out(edge_b1, edge_b, 2, rows_halves)
        sum_0 = summed(mine_0, after(got_0, out_1a))
        total_0 = links.reduce_z(sum_0)
        got_1a = links.swap_x(after(flat(out_1a), got_0))
        got_1b = links.swap_x(after(flat(out_1b), got_1a))
        d_gate = after(d_gate, sum_0)
    grads[2] = product_tn(hidden_low, d_gate)
    d_up_in = after(d_up, grads[2])
    back_part = product_nt((d_gate, w_gate), (d_up_in, w_up))
    if fast:
        back_part = after(back_part, got_1a)
    sends = {}

    def while_reducing(both):
        grads[2] = after(grads[2], both)
        sends["2a"] = cut_out(edge_m, edge_b1, 3, rows_x)
        sends["2b"] = cut_out(edge_a, edge_m, 3, rows_x)
        return (sends["2a"][0], sends["2b"][0], total_0)

    def while_gathering(own):
        sum_1 = summed(mine_1, got_1a, after(got_1b, own))
        sends["outs"] = renew(after(total_0, sum_1), perm, edge_b, held, None)
        sends["1"] = links.reduce_z(sum_1)
        return (sum_1, sends["outs"][0])

    d_hidden = grad_rows + links.reduce_rows(back_part, while_reducing if fast else None)
    if fast:
        got_2a = links.swap_x(after(flat(sends["2a"][0]), got_1a))
        got_2b = links.swap_x(after(flat(sends["2b"][0]), got_2a))
    scaled_a = gain_full[2] * d_hidden
    d_branch = rms_a * scaled_a - branch * rms_a**3 * jnp.mean(scaled_a * branch, axis=-1, keepdims=True)
    d_branch_low = links.gather_rows(d_branch.astype(bf16), while_gathering if fast else None)
    d_attn = product_nt((d_branch_low, w_o))
    if fast:
        total_1, outs = sends["1"], sends["outs"]
    d_qn, d_kn, d_values = attention_back(q_low, k_low, v_low, d_attn, cos_t, sin_t, lengths)
    if fast:
        sum_2a = summed(sends["2a"][1], after(got_2a, d_qn))
        total_2a = links.reduce_z(sum_2a)
        d_qn = after(d_qn, sum_2a, total_1)
    scaled_q = gain_local[0] * d_qn
    scaled_k = gain_local[1] * d_kn
    gain_m_all = jnp.sum(grad_rows * mlp_rows * rms_m, axis=0)
    gain_a_all = jnp.sum(d_hidden * branch * rms_a, axis=0)
    sums = lax.psum(
        jnp.concatenate(
            [
                jnp.sum(scaled_q * queries, axis=-1),
                jnp.sum(scaled_k * keys_raw, axis=-1),
                gain_a_all,
                gain_m_all,
            ]
        ),
        "tensor",
    )
    stat_q, stat_k = sums[:slots], sums[slots : 2 * slots]
    gain_a_all, gain_m_all = sums[2 * slots : 2 * slots + width_d], sums[2 * slots + width_d :]
    d_queries = scale_q * scaled_q - queries * scale_q**3 * (stat_q / width_d)[:, None]
    d_keys = scale_k * scaled_k - keys_raw * scale_k**3 * (stat_k / width_d)[:, None]
    d_qkv = jnp.concatenate([d_queries.astype(bf16), d_keys.astype(bf16), d_values], axis=1)
    grads[4] = product_tn(tok_full, d_qkv)
    grads[3] = product_tn(attn_low, d_branch_low)
    if not fast:
        totals = []
        for lo, hi in ((edge_b, count), (edge_b1, edge_b), (edge_m, edge_b1), (edge_a, edge_m)):
            out_n, mine_n = cut_out(lo, hi, 5, rows_x)
            got_2a = got_2b = links.swap_x(flat(out_n))
            totals.append(links.reduce_z(summed(mine_n, got_2a)))
        total_0, total_1, total_2a, total_2b = totals
        outs = renew(total_0, perm, edge_b, held, None)

    gain_terms = jnp.stack(
        [
            jnp.sum(d_qn * queries * scale_q, axis=0),
            jnp.sum(d_kn * keys_raw * scale_k, axis=0),
            lax.dynamic_slice_in_dim(gain_a_all, links.t * width_local, width_local, 0),
            lax.dynamic_slice_in_dim(gain_m_all, links.t * width_local, width_local, 0),
        ]
    )
    gain_lines = gain_terms.size // size_b
    gain_slot = jnp.pad(gain_terms.reshape(gain_lines, size_b), ((0, size_b - gain_lines), (0, 0))).astype(bf16)
    mid = edge_a // 4 * 2
    turns = list(range(1, links.nz)) + [0]
    first_cut = cut_out(0, edge_a, 5, [[2 * turns[0] + 1], [2 * turns[0]]], gain_slot)
    grads[4] = after(grads[4], first_cut[0])
    rest_rows = [[2 * r + 1] for r in turns[1:]] + [[2 * r for r in turns[1:]]]
    rest = cut_out(0, edge_a, 5, rest_rows, gain_slot)
    rest = list(rest)
    if fast:
        rest[0] = after(rest[0], total_2a)
    to_send = [first_cut[0][0]] + [rest[k][0] for k in range(links.nz - 1)]
    to_keep = [first_cut[1][0]] + [rest[-1][k] for k in range(links.nz - 1)]
    pins = (rest[0],)
    if fast:
        sum_2b = summed(sends["2b"][1], after(got_2b, rest[0]))
        total_2b = links.reduce_z(sum_2b)
        pins = (rest[0], sum_2b)
    outs = renew(total_1, perm, edge_b1, held, outs)
    outs = renew(total_2a, perm, edge_m, held, outs)
    to_send[1] = after(to_send[1], outs[0])

    def joined(kept, got, ring, pins):
        got = after(got, *pins)
        total = kept.astype(f32) + got.astype(f32)
        if ring is not None:
            total = total + after(ring, *pins).astype(f32)
        return total.astype(bf16)

    x_done = [got_2a, got_2b]
    ring = None
    for event in range(links.nz - 2):
        got = links.swap_x(after(to_send[event], x_done[-2]))
        x_done.append(got)
        total = joined(to_keep[event], got, ring, pins)
        ring = links.ring(total)
        pins = ()
        if event == 0:
            input_part = product_nt((after(d_qkv, total), w_qkv))
            pins = (input_part, total_2b)
        if event == links.nz - 3:
            total_at_1 = total
    halves = ((0, mid), (mid, edge_a + 1))
    last_rings = []
    outs = renew(total_2b, perm, edge_a, held, outs)
    to_send[-2] = after(to_send[-2], outs[0])
    fetched = fetch(after(perm, total), edge_a, held)
    to_send[-1] = after(to_send[-1], fetched)
    for lo, hi in halves:
        got = links.swap_x(after(to_send[-2][lo:hi], x_done[-2]))
        x_done.append(got)
        total = joined(to_keep[-2][lo:hi], got, ring[lo:hi], pins)
        last_rings.append(links.ring(total))
        pins = ()
    for (lo, hi), ring in zip(halves, last_rings):
        got = links.swap_x(after(to_send[-1][lo:hi], x_done[-2]))
        x_done.append(got)
        n = min(hi, edge_a) - lo
        total = joined(to_keep[-1][lo : lo + n], got[:n], ring[:n], ())
        outs = renew(total, perm, lo, held, outs, fetched)
    gain_grads = joined(to_keep[-1][edge_a], got[-1], ring[-1], ()).astype(f32)
    gain_grads = gain_grads[:gain_lines].reshape(gain_terms.shape)

    input_rows = links.reduce_rows(after(input_part, total_at_1))
    token_grads = links.rows_to_cols((input_rows + d_hidden).astype(bf16))
    block_out = links.rows_to_cols(after(result, x_done[3]).astype(bf16))

    gain_stats_new = DECAY * gain_stats + (1.0 - DECAY) * gain_grads * gain_grads
    gains_new = gains - GAIN_RATE * gain_grads * gain_roots

    block_grads, left_new, right_new, master_new = (out[None] for out in outs)
    return (
        block_out,
        token_grads,
        block_grads,
        left_new,
        right_new,
        master_new,
        gain_grads,
        gain_stats_new,
        gains_new,
    )


def tile_edges(width_local, width_d, hidden_local, size_b):
    cols_w, cols_h, cols_d = width_local // size_b, hidden_local // size_b, width_d // size_b
    sizes = [cols_d * cols_w] * 4 + [cols_d * cols_h] * 3
    return [sum(sizes[:i]) for i in range(8)], cols_w, cols_h, cols_d


def cut_points(count):
    def at(part):
        return count * part // 128 // 2 * 2

    a, b1, b = at(48), at(84), at(112)
    return {"a": a, "b1": b1, "b": b, "end": count}


def body(
    tokens,
    cotangent,
    lengths,
    gains,
    gain_stats,
    gain_roots,
    master,
    block_order,
    left_stats,
    right_stats,
    left_roots,
    right_roots,
):
    links = Links()
    count, size_b = master.shape[1], master.shape[-1]
    cuts = cut_points(count)
    order = block_order[0].reshape(links.n_dp, count)
    rank = jnp.sum(order[:, None, :] < order[:, :, None], axis=2, dtype=jnp.int32)
    hit = rank[:, None, :] == jnp.arange(count)[None, :, None]
    sorted_ids = jnp.sum(jnp.where(hit, order[:, None, :], 0), axis=2, dtype=jnp.int32)
    rank_own = lax.dynamic_index_in_dim(rank, links.d, 0, False)
    perm = jnp.sum(
        jnp.where(rank_own[None, :] == jnp.arange(count)[:, None], jnp.arange(count)[None, :], 0),
        axis=1,
        dtype=jnp.int32,
    )
    width_local = tokens.shape[1]
    edges = tile_edges(width_local, width_local * links.n_t, FF // links.n_t, size_b)[0]
    counts = jnp.sum(order[:, None, :] < jnp.asarray(edges, jnp.int32)[None, :, None], axis=2, dtype=jnp.int32)
    fits = jnp.all((counts[:, 4] <= cuts["a"]) & (counts[:, 5] <= cuts["b1"]) & (counts[:, 6] <= cuts["b"]))

    table = jnp.concatenate([sorted_ids, counts], axis=1).reshape(links.nz, 2, count + 8)
    table = jnp.where(links.x == 0, table, table[:, ::-1])
    twice = jnp.concatenate([table, table], axis=0)
    ring = lax.dynamic_slice_in_dim(twice, links.z, links.nz, 0)
    table = jnp.concatenate([ring, table], axis=0).reshape(2 * links.n_dp, count + 8)
    tables = (table[:, :count], table[:, count:])
    flag = jnp.broadcast_to(jnp.where(fits, 1.0, 0.0), (1, tokens.shape[1]))
    shared = lax.all_gather(
        jnp.concatenate([gains, flag], axis=0).astype(bf16), "tensor", axis=1, tiled=True
    ).astype(f32)
    gain_full, all_fit = shared[:4], jnp.min(shared[4]) > 0.5
    args = (tokens, cotangent, lengths, gains, gain_stats, gain_roots)
    args = args + (master[0], left_stats[0], right_stats[0], left_roots[0], right_roots[0])

    front = gather_front(links, cuts, tokens, master[0], perm)

    def run(fast):
        return lambda *rest: core(fast, cuts, links, tables, perm, gain_full, front, rest)

    if MODE == "fast":
        return run(True)(*args)
    return lax.cond(all_fit, run(True), run(False), *args)


MODE = "cond"


def solution(mesh):
    placed = (
        P("dp", "tensor"),
        P("dp", "tensor"),
        P("dp"),
        P(None, "tensor"),
        P(None, "tensor"),
        P(None, "tensor"),
        P("tensor", "dp", None, None),
        P("tensor", None),
        P("tensor", "dp", None, None),
        P("tensor", "dp", None, None),
        P("tensor", "dp", None, None),
        P("tensor", "dp", None, None),
    )
    return jax.shard_map(
        body,
        mesh=mesh,
        in_specs=placed,
        out_specs=(
            P("dp", "tensor"),
            P("dp", "tensor"),
            P("tensor", "dp", None, None),
            P("tensor", "dp", None, None),
            P("tensor", "dp", None, None),
            P("tensor", "dp", None, None),
            P(None, "tensor"),
            P(None, "tensor"),
            P(None, "tensor"),
        ),
        check_vma=False,
    )
```

```python
import jax
import jax.numpy as jnp
import numpy as np
from jax import lax
from jax.experimental import pallas as pl
from jax.experimental.pallas import tpu as pltpu
from jax.sharding import PartitionSpec as P

HEADS = 16
HD = 128
FF = 8192
EPSILON = 1e-06
THETA = 500000.0
DECAY = 0.5
LEARN_RATE = 0.25
GAIN_RATE = 0.2
NEG = -1e30
MIB = 1024 * 1024
f32 = jnp.float32
bf16 = jnp.bfloat16


def after(value, *others):
    return lax.optimization_barrier((value,) + others)[0]


class Links:
    def __init__(self):
        self.n_dp = lax.axis_size("dp")
        self.n_t = lax.axis_size("tensor")
        self.nz = self.n_dp // 2
        self.ny = self.n_t // 2
        self.d = lax.axis_index("dp")
        self.z, self.x = self.d // 2, self.d % 2
        self.t = lax.axis_index("tensor")
        self.y, self.c = self.t // 2, self.t % 2
        self.z_groups = [[2 * z + x for z in range(self.nz)] for x in range(2)]

    def ring(self, value):
        pairs = [(2 * z + x, 2 * ((z - 1) % self.nz) + x) for z in range(self.nz) for x in range(2)]
        return lax.ppermute(value, "dp", pairs)

    def gather_z(self, value):
        return lax.all_gather(value, "dp", axis=0, tiled=True, axis_index_groups=self.z_groups)

    def reduce_z(self, value):
        return lax.psum_scatter(
            value, "dp", scatter_dimension=0, tiled=True, axis_index_groups=self.z_groups
        )

    def swap_x(self, value):
        return lax.ppermute(value, "dp", [(i, i ^ 1) for i in range(self.n_dp)])

    def swap_core(self, value):
        return lax.ppermute(value, "tensor", [(i, i ^ 1) for i in range(self.n_t)])

    def shift_y(self, value, step):
        pairs = [(i, 2 * ((i // 2 + step) % self.ny) + i % 2) for i in range(self.n_t)]
        return lax.ppermute(value, "tensor", pairs)

    def shift_t(self, value, step):
        return lax.ppermute(value, "tensor", [(i, (i + step) % self.n_t) for i in range(self.n_t)])

    def gather_rows(self, own, meanwhile=None):
        pieces = [(self.y, own)]
        for step in range(1, self.ny):
            got = self.shift_y(own, step)
            if meanwhile is not None and step == 1:
                got = after(got, *meanwhile(own))
            pieces.append(((self.y + self.ny - step) % self.ny, got))
        parts, places = [], []
        for row_y, piece in pieces:
            parts += [piece, self.swap_core(piece)]
            places += [2 * row_y + self.c, 2 * row_y + 1 - self.c]
        return stack_rows(parts, jnp.stack(places))

    def reduce_rows(self, part, meanwhile=None):
        rows = part.shape[0] // self.n_t
        cut = part.reshape((self.ny, 2, rows, part.shape[1]))
        got = self.swap_core(lax.dynamic_index_in_dim(cut, 1 - self.c, 1, False))
        kept = lax.dynamic_index_in_dim(cut, self.c, 1, False)
        both = (kept.astype(f32) + got.astype(f32)).astype(bf16)
        total = lax.dynamic_index_in_dim(both, self.y, 0, False).astype(f32)
        for step in range(1, self.ny):
            piece = lax.dynamic_index_in_dim(both, (self.y + step) % self.ny, 0, False)
            got = self.shift_y(piece, step)
            if meanwhile is not None and step == 1:
                got = after(got, *meanwhile(both))
            total = total + got.astype(f32)
        return total

    def rows_to_cols(self, own):
        rows, width = own.shape[0], own.shape[1] // self.n_t
        full = jnp.zeros((rows * self.n_t, width), own.dtype)
        for step in range(self.n_t):
            piece = lax.dynamic_slice_in_dim(own, ((self.t + step) % self.n_t) * width, width, 1)
            if step:
                piece = self.shift_t(piece, step)
            row0 = ((self.t + self.n_t - step) % self.n_t) * rows
            full = lax.dynamic_update_slice_in_dim(full, piece, row0, 0)
        return full


def fit(count, most=8):
    return next(step for step in (8, 4, 2, 1) if step <= most and count % step == 0)


def stack_rows(parts, places):
    rows, cols = parts[0].shape
    n = len(parts)

    def kernel(places_ref, *refs):
        out, sem = refs[n], refs[n + 1]
        copies = []
        for i in range(n):
            start = pl.multiple_of(places_ref[i] * rows, rows)
            copies.append(pltpu.make_async_copy(refs[i], out.at[pl.ds(start, rows), :], sem.at[i]))
            copies[-1].start()
        for copy in copies:
            copy.wait()

    return pl.pallas_call(
        kernel,
        grid_spec=pltpu.PrefetchScalarGridSpec(
            num_scalar_prefetch=1,
            grid=(1,),
            in_specs=[pl.BlockSpec(memory_space=pl.ANY)] * n,
            out_specs=pl.BlockSpec(memory_space=pltpu.VMEM),
            scratch_shapes=[pltpu.SemaphoreType.DMA((n,))],
        ),
        out_shape=jax.ShapeDtypeStruct((n * rows, cols), parts[0].dtype),
        compiler_params=pltpu.CompilerParams(vmem_limit_bytes=32 * MIB),
        name="stack_rows",
    )(places, *parts)


def sorted_tiles(master, perm, lo, hi):
    size_b = master.shape[-1]
    step = fit(hi - lo)

    def kernel(perm_ref, *refs):
        for j in range(step):
            refs[step][j] = refs[j][0].astype(bf16)

    def spec(j):
        return pl.BlockSpec((1, size_b, size_b), lambda i, p: (p[lo + step * i + j], 0, 0))

    return pl.pallas_call(
        kernel,
        grid_spec=pltpu.PrefetchScalarGridSpec(
            num_scalar_prefetch=1,
            grid=((hi - lo) // step,),
            in_specs=[spec(j) for j in range(step)],
            out_specs=pl.BlockSpec((step, size_b, size_b), lambda i, p: (i, 0, 0)),
        ),
        out_shape=jax.ShapeDtypeStruct((hi - lo, size_b, size_b), bf16),
        name="sorted_tiles",
    )(perm, *([master] * step))


def place_tiles(sources, parts, shapes, ids, counts, size_b):
    arrays = []
    for source in sources:
        if not any(source[0] is array for array in arrays):
            arrays.append(source[0])
    places = [next(i for i, array in enumerate(arrays) if array is source[0]) for source in sources]
    n_src, n_out = len(arrays), len(shapes)

    def kernel(ids_ref, counts_ref, *refs):
        outs, sem = refs[n_src : n_src + n_out], refs[-1]
        for m, edge, base, cols, off in parts:
            for s, (_, at, row, lo, hi) in zip(places, sources):

                def step(k, carry, s=s, m=m, base=base, cols=cols, off=off, row=row, skip=lo - at):
                    tile = ids_ref[row, k] - base
                    r = tile >> (cols.bit_length() - 1)
                    c = (tile & (cols - 1)) + off
                    pltpu.make_async_copy(
                        refs[s].at[k - skip],
                        outs[m].at[
                            pl.ds(pl.multiple_of(r * size_b, size_b), size_b),
                            pl.ds(pl.multiple_of(c * size_b, size_b), size_b),
                        ],
                        sem,
                    ).start()
                    return carry

                first = jnp.maximum(counts_ref[row, edge], lo)
                last = jnp.minimum(counts_ref[row, edge + 1], hi)
                lax.fori_loop(first, last, step, 0)
        for out in outs:
            pltpu.make_async_copy(out, out, sem).wait()

    return pl.pallas_call(
        kernel,
        grid_spec=pltpu.PrefetchScalarGridSpec(
            num_scalar_prefetch=2,
            grid=(1,),
            in_specs=[pl.BlockSpec(memory_space=pl.ANY)] * n_src,
            out_specs=[pl.BlockSpec(memory_space=pltpu.VMEM)] * n_out,
            scratch_shapes=[pltpu.SemaphoreType.DMA],
        ),
        out_shape=[jax.ShapeDtypeStruct(shape, bf16) for shape in shapes],
        compiler_params=pltpu.CompilerParams(vmem_limit_bytes=60 * MIB),
        name="place_tiles",
    )(ids, counts, *arrays)


def pick_tiles(matrices, parts, ids, counts, rows, lo, hi, size_b, extra=None):
    n_mat, n_out = len(matrices), len(rows)
    more = [] if extra is None else [extra]
    n_src = n_mat + len(more)

    def kernel(ids_ref, counts_ref, *refs):
        outs, sem = refs[n_src : n_src + n_out], refs[-1]
        for m, edge, base, cols, off in parts:
            for i, group in enumerate(rows):
                for j, row in enumerate(group):

                    def step(k, carry, i=i, j=j, row=row, m=m, base=base, cols=cols, off=off):
                        tile = ids_ref[row, k] - base
                        r = tile >> (cols.bit_length() - 1)
                        c = (tile & (cols - 1)) + off
                        pltpu.make_async_copy(
                            refs[m].at[
                                pl.ds(pl.multiple_of(r * size_b, size_b), size_b),
                                pl.ds(pl.multiple_of(c * size_b, size_b), size_b),
                            ],
                            outs[i].at[j, k - lo],
                            sem,
                        ).start()
                        return carry

                    first = jnp.maximum(counts_ref[row, edge], lo)
                    last = jnp.minimum(counts_ref[row, edge + 1], hi)
                    lax.fori_loop(first, last, step, 0)
        if more:
            for i, group in enumerate(rows):
                for j in range(len(group)):
                    pltpu.make_async_copy(refs[n_mat], outs[i].at[j, hi - lo], sem).start()
        for out in outs:
            pltpu.make_async_copy(out, out, sem).wait()

    return pl.pallas_call(
        kernel,
        grid_spec=pltpu.PrefetchScalarGridSpec(
            num_scalar_prefetch=2,
            grid=(1,),
            in_specs=[pl.BlockSpec(memory_space=pl.ANY)] * n_src,
            out_specs=[pl.BlockSpec(memory_space=pltpu.VMEM)] * n_out,
            scratch_shapes=[pltpu.SemaphoreType.DMA],
        ),
        out_shape=[
            jax.ShapeDtypeStruct((len(group), hi - lo + len(more), size_b, size_b), bf16) for group in rows
        ],
        compiler_params=pltpu.CompilerParams(vmem_limit_bytes=60 * MIB),
        name="pick_tiles",
    )(ids, counts, *matrices, *more)


def dot_nt(a, b):
    return lax.dot_general(a, b, (((1,), (1,)), ((), ())), preferred_element_type=f32)


def dot_tn(a, b):
    return lax.dot_general(a, b, (((0,), (0,)), ((), ())), preferred_element_type=f32)


def dot_nn(a, b):
    return lax.dot_general(a, b, (((1,), (0,)), ((), ())), preferred_element_type=f32)


def kept(shape):
    return pl.BlockSpec(shape, lambda i: (0,) * len(shape), pipeline_mode=pl.Buffered(1))


ROOMY = pltpu.CompilerParams(vmem_limit_bytes=52 * MIB)


def product_tn(a, b):
    (rows, m), n = a.shape, b.shape[1]
    step = min(512, m)

    def kernel(a_ref, b_ref, out_ref):
        out_ref[...] = dot_tn(a_ref[...], b_ref[...]).astype(bf16)

    return pl.pallas_call(
        kernel,
        grid=(m // step,),
        in_specs=[pl.BlockSpec((rows, step), lambda i: (0, i)), kept((rows, n))],
        out_specs=pl.BlockSpec((step, n), lambda i: (i, 0)),
        out_shape=jax.ShapeDtypeStruct((m, n), bf16),
        compiler_params=ROOMY,
        name="product_tn",
    )(a, b)


def product_nt(*pairs):
    count, rows, n = len(pairs), pairs[0][0].shape[0], pairs[0][1].shape[0]
    step = min(256, n)

    def kernel(*refs):
        total = dot_nt(refs[0][...], refs[count][...])
        for i in range(1, count):
            total = total + dot_nt(refs[i][...], refs[count + i][...])
        refs[-1][...] = total.astype(bf16)

    return pl.pallas_call(
        kernel,
        grid=(n // step,),
        in_specs=[kept(a.shape) for a, _ in pairs]
        + [pl.BlockSpec((step, b.shape[1]), lambda i: (i, 0)) for _, b in pairs],
        out_specs=pl.BlockSpec((rows, step), lambda i: (0, i)),
        out_shape=jax.ShapeDtypeStruct((rows, n), bf16),
        compiler_params=ROOMY,
        name="product_nt",
    )(*[a for a, _ in pairs], *[b for _, b in pairs])


def inner_back(d_mlp, w_down, gate_act, up_act):
    rows, hidden = gate_act.shape
    step = min(512, hidden)

    def kernel(d_ref, w_ref, gate_ref, up_ref, d_gate_ref, d_up_ref):
        d_inner = dot_nt(d_ref[...], w_ref[...])
        gate = gate_ref[...]
        sig = jax.nn.sigmoid(gate)
        d_gate_ref[...] = (d_inner * up_ref[...] * sig * (1.0 + gate * (1.0 - sig))).astype(bf16)
        d_up_ref[...] = (d_inner * (gate * sig)).astype(bf16)

    strip = pl.BlockSpec((rows, step), lambda i: (0, i))
    return pl.pallas_call(
        kernel,
        grid=(hidden // step,),
        in_specs=[kept(d_mlp.shape), pl.BlockSpec((step, w_down.shape[1]), lambda i: (i, 0)), strip, strip],
        out_specs=[strip, strip],
        out_shape=[jax.ShapeDtypeStruct((rows, hidden), bf16)] * 2,
        compiler_params=ROOMY,
        name="inner_back",
    )(d_mlp, w_down, gate_act, up_act)


def softmax_block(q_block, k_head, first, length):
    keys = k_head.shape[0]
    scores = dot_nt(q_block, k_head) * (HD**-0.5)
    rows = first + lax.broadcasted_iota(jnp.int32, scores.shape, 0)
    cols = lax.broadcasted_iota(jnp.int32, scores.shape, 1)
    scores = jnp.where((cols <= rows) & (cols < length), scores, NEG)
    probs = jnp.exp(scores - jnp.max(scores, axis=-1, keepdims=True))
    return probs / jnp.sum(probs, axis=-1, keepdims=True)


def attention(raw, scale_q, scale_k, gains, cos_t, sin_t, lengths):
    slots, width = raw.shape[0], raw.shape[1] // 3
    heads = width // HD
    block = min(256, slots)

    def kernel(len_ref, q_ref, k_ref, v_ref, sq_ref, sk_ref, gain_ref, cos_ref, sin_ref, out_ref, ql_ref, kl_ref, vl_ref):
        def turned(ref, scale, row):
            val = ref[...] * scale[...] * gain_ref[row : row + 1, :]
            return (val * cos_ref[...] + pltpu.roll(val, HD // 2, 1) * sin_ref[...]).astype(bf16)

        ql_ref[...] = turned(q_ref, sq_ref, 0)
        kl_ref[...] = turned(k_ref, sk_ref, 1)
        vl_ref[...] = v_ref[...].astype(bf16)
        for first in range(0, slots, block):
            last = first + block
            probs = softmax_block(ql_ref[first:last, :], kl_ref[:last, :], first, len_ref[0])
            out_ref[first:last, :] = dot_nn(probs.astype(bf16), vl_ref[:last, :]).astype(bf16)

    def head_spec(part):
        return pl.BlockSpec((slots, HD), lambda h, n: (0, part * heads + h))

    whole = lambda shape: pl.BlockSpec(shape, lambda h, n: (0, 0))
    out_spec = pl.BlockSpec((slots, HD), lambda h, n: (0, h))
    return pl.pallas_call(
        kernel,
        grid_spec=pltpu.PrefetchScalarGridSpec(
            num_scalar_prefetch=1,
            grid=(heads,),
            in_specs=[head_spec(0), head_spec(1), head_spec(2), whole((slots, 1)), whole((slots, 1))]
            + [pl.BlockSpec((4, HD), lambda h, n: (0, h)), whole((slots, HD)), whole((slots, HD))],
            out_specs=[out_spec] * 4,
        ),
        out_shape=[jax.ShapeDtypeStruct((slots, width), bf16)] * 4,
        compiler_params=pltpu.CompilerParams(vmem_limit_bytes=48 * MIB),
        name="attention",
    )(lengths, raw, raw, raw, scale_q, scale_k, gains, cos_t, sin_t)


def attention_back(q_low, k_low, v_low, d_attn, cos_t, sin_t, lengths):
    slots, width = q_low.shape
    heads = width // HD
    block = min(256, slots)

    def kernel(len_ref, q_ref, k_ref, v_ref, do_ref, cos_ref, sin_ref, dq_ref, dk_ref, dv_ref, dk_acc, dv_acc):
        def turned_back(val, rows):
            return val * cos_ref[rows, :] - pltpu.roll(val, HD // 2, 1) * sin_ref[rows, :]

        dk_acc[...] = jnp.zeros_like(dk_acc)
        dv_acc[...] = jnp.zeros_like(dv_acc)
        for first in range(0, slots, block):
            last = first + block
            rows, keys = slice(first, last), slice(0, last)
            probs = softmax_block(q_ref[rows, :], k_ref[keys, :], first, len_ref[0])
            d_out = do_ref[rows, :]
            d_probs = dot_nt(d_out, v_ref[keys, :])
            delta = jnp.sum(probs * d_probs, axis=-1, keepdims=True)
            d_scores = (probs * (d_probs - delta)).astype(bf16)
            dq_ref[rows, :] = turned_back(dot_nn(d_scores, k_ref[keys, :]) * (HD**-0.5), rows)
            dk_acc[keys, :] += dot_tn(d_scores, q_ref[rows, :])
            dv_acc[keys, :] += dot_tn(probs.astype(bf16), d_out)
        dk_ref[...] = turned_back(dk_acc[...] * (HD**-0.5), slice(0, slots))
        dv_ref[...] = dv_acc[...].astype(bf16)

    spec = pl.BlockSpec((slots, HD), lambda h, n: (0, h))
    whole = pl.BlockSpec((slots, HD), lambda h, n: (0, 0))
    return pl.pallas_call(
        kernel,
        grid_spec=pltpu.PrefetchScalarGridSpec(
            num_scalar_prefetch=1,
            grid=(heads,),
            in_specs=[spec] * 4 + [whole] * 2,
            out_specs=[spec] * 3,
            scratch_shapes=[pltpu.VMEM((slots, HD), f32)] * 2,
        ),
        out_shape=[
            jax.ShapeDtypeStruct((slots, width), f32),
            jax.ShapeDtypeStruct((slots, width), f32),
            jax.ShapeDtypeStruct((slots, width), bf16),
        ],
        compiler_params=pltpu.CompilerParams(vmem_limit_bytes=48 * MIB),
        name="attention_back",
    )(lengths, q_low, k_low, v_low, d_attn, cos_t, sin_t)


def renew(grads, perm, lo, held, outs, fetched=None):
    count, size_b = grads.shape[0], grads.shape[-1]
    n_old = 0 if outs is None else len(outs)
    batch = fit(count)
    steps = count // batch

    n_in = 5 * batch if fetched is None else 1

    def kernel(perm_ref, g_ref, *refs):
        outs_ref = refs[n_in + n_old : n_in + n_old + 4]
        held_ref, sems = refs[-2:]
        i = pl.program_id(0)
        side = i % 2

        def drain(which):
            pltpu.make_async_copy(held_ref.at[which], held_ref.at[which], sems.at[which]).wait()

        @pl.when(i >= 2)
        def _():
            drain(side)

        for j in range(batch):
            if fetched is None:
                tiles = [refs[a * batch + j][0] for a in range(5)]
            else:
                tiles = [refs[0][j, a] for a in range(5)]
            master, left_s, right_s, left_r, right_r = tiles
            g = g_ref[j]
            held_ref[side, 0, j] = g.astype(f32)
            held_ref[side, 1, j] = DECAY * left_s + (1.0 - DECAY) * dot_nt(g, g)
            held_ref[side, 2, j] = DECAY * right_s + (1.0 - DECAY) * dot_tn(g, g)
            left = dot_nn(left_r.astype(bf16), g).astype(bf16)
            held_ref[side, 3, j] = master - LEARN_RATE * dot_nn(left, right_r.astype(bf16))
        for j in range(batch):
            slot = perm_ref[lo + batch * i + j]
            for a in range(4):
                pltpu.make_async_copy(held_ref.at[side, a, j], outs_ref[a].at[slot], sems.at[side]).start()

        @pl.when(i == steps - 1)
        def _():
            drain(side)
            if steps > 1:
                drain(1 - side)

    def spec(j):
        return pl.BlockSpec((1, size_b, size_b), lambda i, p: (p[lo + batch * i + j], 0, 0))

    return pl.pallas_call(
        kernel,
        grid_spec=pltpu.PrefetchScalarGridSpec(
            num_scalar_prefetch=1,
            grid=(steps,),
            in_specs=[pl.BlockSpec((batch, size_b, size_b), lambda i, p: (i, 0, 0))]
            + (
                [spec(j) for _ in range(5) for j in range(batch)]
                if fetched is None
                else [pl.BlockSpec((batch, 5, size_b, size_b), lambda i, p: (lo // batch + i, 0, 0, 0))]
            )
            + [pl.BlockSpec(memory_space=pl.ANY)] * n_old,
            out_specs=[pl.BlockSpec(memory_space=pl.ANY)] * 4,
            scratch_shapes=[
                pltpu.VMEM((2, 4, batch, size_b, size_b), f32),
                pltpu.SemaphoreType.DMA((2,)),
            ],
        ),
        out_shape=[jax.ShapeDtypeStruct(held[0].shape, f32)] * 4,
        input_output_aliases={2 + n_in + i: i for i in range(n_old)},
        compiler_params=pltpu.CompilerParams(vmem_limit_bytes=40 * MIB),
        name="renew",
    )(perm, grads, *([array for array in held for _ in range(batch)] if fetched is None else [fetched]), *(outs or ()))


def fetch(perm, count, held):
    size_b = held[0].shape[-1]

    def kernel(perm_ref, *refs):
        out, sem = refs[-2:]

        def step(k, carry):
            slot = perm_ref[k]
            for a in range(5):
                pltpu.make_async_copy(refs[a].at[slot], out.at[k, a], sem).start()
            return carry

        lax.fori_loop(0, count, step, 0)
        pltpu.make_async_copy(out, out, sem).wait()

    return pl.pallas_call(
        kernel,
        grid_spec=pltpu.PrefetchScalarGridSpec(
            num_scalar_prefetch=1,
            grid=(1,),
            in_specs=[pl.BlockSpec(memory_space=pl.ANY)] * 5,
            out_specs=pl.BlockSpec(memory_space=pltpu.VMEM),
            scratch_shapes=[pltpu.SemaphoreType.DMA],
        ),
        out_shape=jax.ShapeDtypeStruct((count, 5, size_b, size_b), f32),
        compiler_params=pltpu.CompilerParams(vmem_limit_bytes=40 * MIB),
        name="fetch",
    )(perm, *held)


def rope_tables(seq_len):
    half = HD // 2
    freqs = THETA ** (-(2.0 * jnp.arange(half, dtype=f32)) / HD)
    angles = jnp.arange(seq_len, dtype=f32)[:, None] * freqs[None, :]
    cos_t, sin_t = jnp.cos(angles), jnp.sin(angles)
    return jnp.concatenate([cos_t, cos_t], 1), jnp.concatenate([-sin_t, sin_t], 1)


def gather_front(links, cuts, tokens, master, perm):
    edge_a, edge_b1, edge_b, count = cuts["a"], cuts["b1"], cuts["b"], cuts["end"]
    own_a = sorted_tiles(master, perm, 0, edge_a)
    later = after(perm, own_a)
    owns = [sorted_tiles(master, later, lo, hi) for lo, hi in ((edge_a, edge_b1), (edge_b1, edge_b), (edge_b, count))]
    tok_full = lax.all_gather(tokens, "tensor", axis=1, tiled=True)
    return owns, own_a, links.swap_x(own_a), links.ring(own_a), tok_full


def core(fast, cuts, links, tables, perm, gain_full, front, args):
    tokens, cotangent, lengths, gains, gain_stats, gain_roots = args[:6]
    master, left_stats, right_stats, left_roots, right_roots = args[6:]
    ids, counts = tables
    size_b = master.shape[-1]
    slots, width_local = tokens.shape
    n_t = links.n_t
    width_d = width_local * n_t
    hidden_local = FF // n_t
    count = master.shape[0]

    edges, cols_w, cols_h, cols_d = tile_edges(width_local, width_d, hidden_local, size_b)
    qkv_parts = [(i, edges[i], cols_w, i * cols_w) for i in range(3)]
    o_part, gate_part, up_part, down_part = (
        (3 + i, edges[3 + i], cols, 0) for i, cols in enumerate((cols_d, cols_h, cols_h, cols_d))
    )

    edge_a, edge_b1, edge_b, count = cuts["a"], cuts["b1"], cuts["b"], cuts["end"]
    owns, own_a, their_a, next_a, tok_full = front
    mine, theirs = [own_a, next_a], [their_a]
    for r in range(2, links.nz):
        mine.append(links.ring(after(mine[-1], theirs[r - 2])))
        theirs.append(links.swap_x(after(mine[r - 1], theirs[-1])))
    theirs.append(links.swap_x(after(mine[-1], theirs[-1])))
    own_b1 = links.swap_x(after(owns[0], theirs[-1]))
    own_c = links.swap_x(after(owns[2], own_b1))
    own_b2 = links.swap_x(after(owns[1], own_b1))
    cot_full = lax.all_gather(cotangent, "tensor", axis=1, tiled=True)
    sources_a = []
    for r in range(links.nz):
        sources_a.append((mine[r], 0, 2 * r, 0, edge_a))
        sources_a.append((theirs[r], 0, 2 * r + 1, 0, edge_a))

    def matrices(sources, groups, shapes):
        return place_tiles(sources, [(m,) + part for m, part in groups], shapes, ids, counts, size_b)

    def others(gathered, n):
        return [
            lax.dynamic_slice_in_dim(gathered, ((links.z + r) % links.nz) * n, n, 0) for r in range(1, links.nz)
        ]

    def send_others(pieces, last):
        sent = []
        for piece in pieces:
            last = links.swap_x(after(piece, last))
            sent.append(last)
        return sent

    def all_sources(lo, hi, gathered, own_x, rest_x):
        n = hi - lo
        found = [(gathered, z * n, links.n_dp + 2 * z, lo, hi) for z in range(links.nz)]
        found.append((own_x, 0, 1, lo, hi))
        return found + [(rest_x[r - 1], 0, 2 * r + 1, lo, hi) for r in range(1, links.nz)]

    n_b1, n_b2, n_c = edge_b1 - edge_a, edge_b - edge_b1, count - edge_b
    z_b1, z_b2, z_c = (
        links.gather_z(after(own, mine[-1], theirs[-2])) for own in (owns[0], owns[1], jnp.concatenate([owns[2], own_c], axis=0))
    )
    pieces_b1 = others(z_b1, n_b1)
    rest_b1 = send_others(pieces_b1, own_b2)
    rest_b2 = send_others(others(z_b2, n_b2), rest_b1[-1])
    sources_b1 = sources_a + all_sources(edge_a, edge_b1, z_b1, own_b1, rest_b1)
    sources_b2 = sources_b1 + all_sources(edge_b1, edge_b, z_b2, own_b2, rest_b2)
    sources_c = sources_b2 + [
        (z_c, (2 * z + xr) * n_c, links.n_dp + 2 * z + xr, edge_b, count) for z in range(links.nz) for xr in range(2)
    ]
    if not fast:
        sources_a = sources_b1 = sources_b2 = sources_c

    gain_local = gains.astype(bf16).astype(f32)
    length = lengths[0]
    cos_t, sin_t = rope_tables(slots)
    own_rows = slots // n_t
    row0 = links.t * own_rows
    tok_rows = lax.dynamic_slice_in_dim(tok_full, row0, own_rows, 0).astype(f32)
    live = (row0 + jnp.arange(own_rows) < length).astype(f32)[:, None]
    grad_rows = lax.dynamic_slice_in_dim(cot_full, row0, own_rows, 0).astype(f32) * live

    w_qkv, w_o = matrices(
        sources_a,
        [(0, part) for part in qkv_parts] + [(1, o_part)],
        [(width_d, 3 * width_local), (width_local, width_d)],
    )
    raw = after(dot_nn(tok_full, w_qkv), own_b1)
    queries, keys_raw = raw[:, :width_local], raw[:, width_local : 2 * width_local]
    squares = lax.psum(
        jnp.stack([jnp.sum(queries * queries, axis=-1), jnp.sum(keys_raw * keys_raw, axis=-1)]), "tensor"
    )
    scale_q = lax.rsqrt(squares[0] / width_d + EPSILON)[:, None]
    scale_k = lax.rsqrt(squares[1] / width_d + EPSILON)[:, None]
    attn_low, q_low, k_low, v_low = attention(raw, scale_q, scale_k, gain_local, cos_t, sin_t, lengths)
    branch = links.reduce_rows(dot_nn(after(attn_low, own_c, own_b2, pieces_b1[0]), w_o).astype(bf16))
    rms_a = lax.rsqrt(jnp.mean(branch * branch, axis=-1, keepdims=True) + EPSILON)
    hidden_rows = tok_rows + branch * rms_a * gain_full[2]
    hidden_low = links.gather_rows(hidden_rows.astype(bf16))
    hidden_low = after(hidden_low, rest_b1[0])

    (w_gate,) = matrices(sources_b1, [(0, gate_part)], [(width_d, hidden_local)])
    gate_act = dot_nn(hidden_low, w_gate)
    sig_gate = jax.nn.sigmoid(gate_act)
    silu_act = gate_act * sig_gate
    (w_down,) = matrices(sources_c, [(0, down_part)], [(hidden_local, width_d)])
    sources_b2 = [(after(sources_b2[0][0], w_down),) + sources_b2[0][1:]] + sources_b2[1:]
    (w_up,) = matrices(sources_b2, [(0, up_part)], [(width_d, hidden_local)])
    up_act = dot_nn(hidden_low, w_up)
    inner_low = (silu_act * up_act).astype(bf16)
    mlp_rows = links.reduce_rows(dot_nn(inner_low, w_down).astype(bf16))
    rms_m = lax.rsqrt(jnp.mean(mlp_rows * mlp_rows, axis=-1, keepdims=True) + EPSILON)
    result = hidden_rows + mlp_rows * rms_m * gain_full[3]
    scaled_m = gain_full[3] * grad_rows
    d_mlp = rms_m * scaled_m - mlp_rows * rms_m**3 * jnp.mean(scaled_m * mlp_rows, axis=-1, keepdims=True)
    d_mlp_low = links.gather_rows(d_mlp.astype(bf16))

    grads = {}
    grad_parts = [(0, down_part), (1, up_part), (2, gate_part), (3, o_part)] + [(4, p) for p in qkv_parts]
    held = (master, left_stats, right_stats, left_roots, right_roots)
    edge_m = (edge_a + edge_b1) // 4 * 2
    rows_x = [[links.n_dp + 2 * z + xr for z in range(links.nz)] for xr in (1, 0)]
    half_z = links.nz // 2
    rows_halves = [rows_x[0][:half_z], rows_x[0][half_z:], rows_x[1]]

    def cut_out(lo, hi, n_mats, rows, extra=None):
        parts = [(m,) + part for m, part in grad_parts if m < n_mats]
        return pick_tiles([grads[m] for m in range(n_mats)], parts, ids, counts, rows, lo, hi, size_b, extra)

    def flat(value):
        return value.reshape((-1, size_b, size_b))

    def summed(mine, *got):
        return (flat(mine).astype(f32) + jnp.concatenate(got, axis=0).astype(f32)).astype(bf16)

    grads[0] = product_tn(inner_low, d_mlp_low)
    if fast:
        out_0, mine_0 = cut_out(edge_b, count, 1, rows_x)
        got_0 = links.swap_x(flat(out_0))
        d_mlp_low = after(d_mlp_low, out_0)
    d_gate, d_up = inner_back(d_mlp_low, w_down, gate_act, up_act)
    grads[1] = product_tn(hidden_low, d_up)
    if fast:
        out_1a, out_1b, mine_1 = cut_out(edge_b1, edge_b, 2, rows_halves)
        sum_0 = summed(mine_0, after(got_0, out_1a))
        total_0 = links.reduce_z(sum_0)
        got_1a = links.swap_x(after(flat(out_1a), got_0))
        got_1b = links.swap_x(after(flat(out_1b), got_1a))
        d_gate = after(d_gate, sum_0)
    grads[2] = product_tn(hidden_low, d_gate)
    d_up_in = after(d_up, grads[2])
    back_part = product_nt((d_gate, w_gate), (d_up_in, w_up))
    if fast:
        back_part = after(back_part, got_1a)
    sends = {}

    def while_reducing(both):
        grads[2] = after(grads[2], both)
        sends["2a"] = cut_out(edge_m, edge_b1, 3, rows_x)
        sends["2b"] = cut_out(edge_a, edge_m, 3, rows_x)
        return (sends["2a"][0], sends["2b"][0], total_0)

    def while_gathering(own):
        sum_1 = summed(mine_1, got_1a, after(got_1b, own))
        sends["outs"] = renew(after(total_0, sum_1), perm, edge_b, held, None)
        sends["1"] = links.reduce_z(sum_1)
        return (sum_1, sends["outs"][0])

    d_hidden = grad_rows + links.reduce_rows(back_part, while_reducing if fast else None)
    if fast:
        got_2a = links.swap_x(after(flat(sends["2a"][0]), got_1a))
        got_2b = links.swap_x(after(flat(sends["2b"][0]), got_2a))
    scaled_a = gain_full[2] * d_hidden
    d_branch = rms_a * scaled_a - branch * rms_a**3 * jnp.mean(scaled_a * branch, axis=-1, keepdims=True)
    d_branch_low = links.gather_rows(d_branch.astype(bf16), while_gathering if fast else None)
    d_attn = product_nt((d_branch_low, w_o))
    if fast:
        total_1, outs = sends["1"], sends["outs"]
    d_qn, d_kn, d_values = attention_back(q_low, k_low, v_low, d_attn, cos_t, sin_t, lengths)
    if fast:
        sum_2a = summed(sends["2a"][1], after(got_2a, d_qn))
        total_2a = links.reduce_z(sum_2a)
        d_qn = after(d_qn, sum_2a, total_1)
    scaled_q = gain_local[0] * d_qn
    scaled_k = gain_local[1] * d_kn
    gain_m_all = jnp.sum(grad_rows * mlp_rows * rms_m, axis=0)
    gain_a_all = jnp.sum(d_hidden * branch * rms_a, axis=0)
    sums = lax.psum(
        jnp.concatenate(
            [
                jnp.sum(scaled_q * queries, axis=-1),
                jnp.sum(scaled_k * keys_raw, axis=-1),
                gain_a_all,
                gain_m_all,
            ]
        ),
        "tensor",
    )
    stat_q, stat_k = sums[:slots], sums[slots : 2 * slots]
    gain_a_all, gain_m_all = sums[2 * slots : 2 * slots + width_d], sums[2 * slots + width_d :]
    d_queries = scale_q * scaled_q - queries * scale_q**3 * (stat_q / width_d)[:, None]
    d_keys = scale_k * scaled_k - keys_raw * scale_k**3 * (stat_k / width_d)[:, None]
    d_qkv = jnp.concatenate([d_queries.astype(bf16), d_keys.astype(bf16), d_values], axis=1)
    grads[4] = product_tn(tok_full, d_qkv)
    grads[3] = product_tn(attn_low, d_branch_low)
    if not fast:
        totals = []
        for lo, hi in ((edge_b, count), (edge_b1, edge_b), (edge_m, edge_b1), (edge_a, edge_m)):
            out_n, mine_n = cut_out(lo, hi, 5, rows_x)
            got_2a = got_2b = links.swap_x(flat(out_n))
            totals.append(links.reduce_z(summed(mine_n, got_2a)))
        total_0, total_1, total_2a, total_2b = totals
        outs = renew(total_0, perm, edge_b, held, None)

    gain_terms = jnp.stack(
        [
            jnp.sum(d_qn * queries * scale_q, axis=0),
            jnp.sum(d_kn * keys_raw * scale_k, axis=0),
            lax.dynamic_slice_in_dim(gain_a_all, links.t * width_local, width_local, 0),
            lax.dynamic_slice_in_dim(gain_m_all, links.t * width_local, width_local, 0),
        ]
    )
    gain_lines = gain_terms.size // size_b
    gain_slot = jnp.pad(gain_terms.reshape(gain_lines, size_b), ((0, size_b - gain_lines), (0, 0))).astype(bf16)
    mid = edge_a // 4 * 2
    turns = list(range(1, links.nz)) + [0]
    first_cut = cut_out(0, edge_a, 5, [[2 * turns[0] + 1], [2 * turns[0]]], gain_slot)
    grads[4] = after(grads[4], first_cut[0])
    rest_rows = [[2 * r + 1] for r in turns[1:]] + [[2 * r for r in turns[1:]]]
    rest = cut_out(0, edge_a, 5, rest_rows, gain_slot)
    rest = list(rest)
    if fast:
        rest[0] = after(rest[0], total_2a)
    to_send = [first_cut[0][0]] + [rest[k][0] for k in range(links.nz - 1)]
    to_keep = [first_cut[1][0]] + [rest[-1][k] for k in range(links.nz - 1)]
    pins = (rest[0],)
    if fast:
        sum_2b = summed(sends["2b"][1], after(got_2b, rest[0]))
        total_2b = links.reduce_z(sum_2b)
        pins = (rest[0], sum_2b)
    outs = renew(total_1, perm, edge_b1, held, outs)
    outs = renew(total_2a, perm, edge_m, held, outs)
    to_send[1] = after(to_send[1], outs[0])

    def joined(kept, got, ring, pins):
        got = after(got, *pins)
        total = kept.astype(f32) + got.astype(f32)
        if ring is not None:
            total = total + after(ring, *pins).astype(f32)
        return total.astype(bf16)

    x_done = [got_2a, got_2b]
    ring = None
    for event in range(links.nz - 2):
        got = links.swap_x(after(to_send[event], x_done[-2]))
        x_done.append(got)
        total = joined(to_keep[event], got, ring, pins)
        ring = links.ring(total)
        pins = ()
        if event == 0:
            input_part = product_nt((after(d_qkv, total), w_qkv))
            outs = renew(after(total_2b, input_part), perm, edge_a, held, outs)
            fetched = fetch(after(perm, outs[0]), edge_a, held)
            pins = (input_part, outs[0], fetched)
        if event == links.nz - 3:
            total_at_1 = total
    halves = ((0, mid), (mid, edge_a + 1))
    last_rings = []
    for lo, hi in halves:
        got = links.swap_x(after(to_send[-2][lo:hi], x_done[-2]))
        x_done.append(got)
        total = joined(to_keep[-2][lo:hi], got, ring[lo:hi], pins)
        last_rings.append(links.ring(total))
        pins = ()
    for (lo, hi), ring in zip(halves, last_rings):
        got = links.swap_x(after(to_send[-1][lo:hi], x_done[-2]))
        x_done.append(got)
        n = min(hi, edge_a) - lo
        total = joined(to_keep[-1][lo : lo + n], got[:n], ring[:n], ())
        outs = renew(total, perm, lo, held, outs, fetched)
    gain_grads = joined(to_keep[-1][edge_a], got[-1], ring[-1], ()).astype(f32)
    gain_grads = gain_grads[:gain_lines].reshape(gain_terms.shape)

    input_rows = links.reduce_rows(after(input_part, total_at_1))
    token_grads = links.rows_to_cols((input_rows + d_hidden).astype(bf16))
    block_out = links.rows_to_cols(after(result, x_done[3]).astype(bf16))

    gain_stats_new = DECAY * gain_stats + (1.0 - DECAY) * gain_grads * gain_grads
    gains_new = gains - GAIN_RATE * gain_grads * gain_roots

    block_grads, left_new, right_new, master_new = (out[None] for out in outs)
    return (
        block_out,
        token_grads,
        block_grads,
        left_new,
        right_new,
        master_new,
        gain_grads,
        gain_stats_new,
        gains_new,
    )


def tile_edges(width_local, width_d, hidden_local, size_b):
    cols_w, cols_h, cols_d = width_local // size_b, hidden_local // size_b, width_d // size_b
    sizes = [cols_d * cols_w] * 4 + [cols_d * cols_h] * 3
    return [sum(sizes[:i]) for i in range(8)], cols_w, cols_h, cols_d


def cut_points(count):
    def at(part):
        return count * part // 128 // 2 * 2

    a, b1, b = at(48), at(84), at(112)
    return {"a": a, "b1": b1, "b": b, "end": count}


def body(
    tokens,
    cotangent,
    lengths,
    gains,
    gain_stats,
    gain_roots,
    master,
    block_order,
    left_stats,
    right_stats,
    left_roots,
    right_roots,
):
    links = Links()
    count, size_b = master.shape[1], master.shape[-1]
    cuts = cut_points(count)
    order = block_order[0].reshape(links.n_dp, count)
    rank = jnp.sum(order[:, None, :] < order[:, :, None], axis=2, dtype=jnp.int32)
    hit = rank[:, None, :] == jnp.arange(count)[None, :, None]
    sorted_ids = jnp.sum(jnp.where(hit, order[:, None, :], 0), axis=2, dtype=jnp.int32)
    rank_own = lax.dynamic_index_in_dim(rank, links.d, 0, False)
    perm = jnp.sum(
        jnp.where(rank_own[None, :] == jnp.arange(count)[:, None], jnp.arange(count)[None, :], 0),
        axis=1,
        dtype=jnp.int32,
    )
    width_local = tokens.shape[1]
    edges = tile_edges(width_local, width_local * links.n_t, FF // links.n_t, size_b)[0]
    counts = jnp.sum(order[:, None, :] < jnp.asarray(edges, jnp.int32)[None, :, None], axis=2, dtype=jnp.int32)
    fits = jnp.all((counts[:, 4] <= cuts["a"]) & (counts[:, 5] <= cuts["b1"]) & (counts[:, 6] <= cuts["b"]))

    table = jnp.concatenate([sorted_ids, counts], axis=1).reshape(links.nz, 2, count + 8)
    table = jnp.where(links.x == 0, table, table[:, ::-1])
    twice = jnp.concatenate([table, table], axis=0)
    ring = lax.dynamic_slice_in_dim(twice, links.z, links.nz, 0)
    table = jnp.concatenate([ring, table], axis=0).reshape(2 * links.n_dp, count + 8)
    tables = (table[:, :count], table[:, count:])
    flag = jnp.broadcast_to(jnp.where(fits, 1.0, 0.0), (1, tokens.shape[1]))
    shared = lax.all_gather(
        jnp.concatenate([gains, flag], axis=0).astype(bf16), "tensor", axis=1, tiled=True
    ).astype(f32)
    gain_full, all_fit = shared[:4], jnp.min(shared[4]) > 0.5
    args = (tokens, cotangent, lengths, gains, gain_stats, gain_roots)
    args = args + (master[0], left_stats[0], right_stats[0], left_roots[0], right_roots[0])

    front = gather_front(links, cuts, tokens, master[0], perm)

    def run(fast):
        return lambda *rest: core(fast, cuts, links, tables, perm, gain_full, front, rest)

    if MODE == "fast":
        return run(True)(*args)
    return lax.cond(all_fit, run(True), run(False), *args)


MODE = "cond"


def solution(mesh):
    placed = (
        P("dp", "tensor"),
        P("dp", "tensor"),
        P("dp"),
        P(None, "tensor"),
        P(None, "tensor"),
        P(None, "tensor"),
        P("tensor", "dp", None, None),
        P("tensor", None),
        P("tensor", "dp", None, None),
        P("tensor", "dp", None, None),
        P("tensor", "dp", None, None),
        P("tensor", "dp", None, None),
    )
    return jax.shard_map(
        body,
        mesh=mesh,
        in_specs=placed,
        out_specs=(
            P("dp", "tensor"),
            P("dp", "tensor"),
            P("tensor", "dp", None, None),
            P("tensor", "dp", None, None),
            P("tensor", "dp", None, None),
            P("tensor", "dp", None, None),
            P(None, "tensor"),
            P(None, "tensor"),
            P(None, "tensor"),
        ),
        check_vma=False,
    )
```
